256 devices in a mesh: ctx: 32 (over x, z), voc: 8 (over y, core).
Axes of the slice: x: 4, y: 4, z: 8, core: 2. Of those that a mesh axis runs over, the one named last changes fastest.
Arguments:
- hidden: bfloat16 [4096, 896], P('ctx')
- token_weight: bfloat16 [4096], P('ctx'), may hold values from 1 to 16
- head_weight: bfloat16 [896, 131072], P(None, ('ctx', 'voc'))
- teacher_logits: bfloat16 [4096, 65536], P('ctx', 'voc')
- block_coeff: bfloat16 [512, 128, 128], P('voc')
- block_map: int32 [512], replicated, may hold values from 0 to 1023, as said below
Outputs:
- grad_hidden: bfloat16 [4096, 896], P('ctx')
- grad_weight: float32 [896, 131072], P(None, ('ctx', 'voc'))
- row_loss: float32 [4096], P('ctx')
The draws below stay inside these ranges and needn't reach their ends.
Inputs may be any that keep to these rules, and one draw needn't show every extreme that they name: `block_map`: student block s belongs to voc index (s // 4) modulo the number of voc indices, and teacher block b to voc index b // 64. Of the 64 teacher blocks of one voc index, at most 16 map into the student blocks of any one voc index; in every draw one voc index receives exactly 16 from every voc index.
All inputs are finite; a program needn't handle non-finite values.
Results may differ from the reference program's by a relative error of at most 0.014.
Values may be sent and summed in bfloat16 or wider, within the bound.
No kernel may reach another device: no remote copies, remote signals or barrier semaphores. Data moves between devices by JAX's collectives and lax.ppermute only.
A program may use at most 192 MiB of HBM per device.

```python
import math
import jax
import jax.numpy as jnp
from jax import lax

D = 896
VS = 131072
TV = 65536
BLK = 128
TOKENS = 4096
HALF = 64
TVB = 512
VSB = 1024
CAP = 16
N_CTX = 32
N_VOC = 8


def scales(key, length, lower_end, upper_end):
    return jnp.exp(jax.random.uniform(key, (length,), jnp.float32, jnp.log(lower_end), jnp.log(upper_end)))


def draw_hidden(key, part):
    key = jax.random.fold_in(key, 21)
    base_key, scale_key = jax.random.split(key)
    row_scale = scales(scale_key, TOKENS, 0.3, 3.0)
    values = jax.random.normal(base_key, (TOKENS, D), jnp.float32) * row_scale[:, None]
    return values.astype(jnp.bfloat16)


def draw_head_weight(key, part):
    key = jax.random.fold_in(key, 22)
    base_key, scale_key = jax.random.split(key)
    col_rise = 1.0 + jnp.arange(VS, dtype=jnp.float32) / VS
    col_scale = scales(scale_key, VS, 0.4, 1.2) * col_rise
    weight = jax.random.normal(base_key, (D, VS), jnp.float32) * col_scale[None, :] / jnp.sqrt(jnp.float32(D))
    return weight.astype(jnp.bfloat16)


def draw_teacher_logits(key, part):
    key = jax.random.fold_in(key, 23)
    base_key, row_key, col_key = jax.random.split(key, 3)
    col_shift = jnp.log(3.0) * jnp.arange(TV, dtype=jnp.float32) / TV
    row_scale = scales(row_key, TOKENS, 0.25, 2.5)
    col_scale = scales(col_key, TV, 0.5, 1.5)
    values = jax.random.normal(base_key, (TOKENS, TV), jnp.float32) * row_scale[:, None] * col_scale[None, :] + col_shift[None, :]
    return values.astype(jnp.bfloat16)


def draw_block_coeff(key, part):
    key = jax.random.fold_in(key, 24)
    diag_key, off_key = jax.random.split(key)
    identity = jnp.arange(BLK)[:, None] == jnp.arange(BLK)[None, :]
    diagonal = jax.random.uniform(diag_key, (TVB, BLK, BLK), jnp.float32, 0.5, 1.5)
    off_diag = jax.random.uniform(off_key, (TVB, BLK, BLK), jnp.float32, 0.0, 2.0 / BLK)
    return jnp.where(identity[None, :, :], diagonal, off_diag).astype(jnp.bfloat16)


def draw_block_map(key, part):
    key = jax.random.fold_in(key, 25)
    hot_key, order_key, slot_key = jax.random.split(key, 3)
    local_count = TVB // N_VOC
    dev_blocks = VSB // (N_CTX * N_VOC)
    hot_voc = jax.random.randint(hot_key, (), 0, N_VOC)
    order_keys = jax.random.split(order_key, N_VOC)
    position = jax.vmap(lambda one_key: jax.random.permutation(one_key, local_count))(order_keys)
    spread = (hot_voc + 1 + (position - CAP) % (N_VOC - 1)) % N_VOC
    owner = jnp.where(position < CAP, hot_voc, spread)
    within = jax.random.randint(slot_key, (N_VOC, local_count), 0, N_CTX * dev_blocks)
    block_ids = within // dev_blocks * (N_VOC * dev_blocks) + owner * dev_blocks + within % dev_blocks
    return block_ids.reshape(TVB).astype(jnp.int32)


def steps_of(stream_key, dims, cuts, low, largest):
    gain, own = 1.0, jax.random.fold_in(stream_key, 6)
    for dim, blocks in cuts:
        steps = jnp.exp(jax.random.uniform(jax.random.fold_in(own, dim), (blocks,), jnp.float32, low / len(cuts), largest / len(cuts)))
        gain = gain * jnp.repeat(steps, dims[dim] // blocks).reshape([-1 if axis == dim else 1 for axis in range(len(dims))])
    return gain


def setup_inputs(seed: int = 0) -> dict:
    splits = jax.random.split(jax.random.key(seed), 7)
    hidden = draw_hidden(jax.random.fold_in(splits[6], 71), 0)
    token_weight = jnp.clip(jnp.exp(math.log(16.0) - 2.7725887 * jax.random.uniform(splits[1], (TOKENS,), jnp.float32) ** steps_of(splits[1], (TOKENS,), ((0, 32),), -0.2, 0.2)), 1.0, 16.0).astype(jnp.bfloat16)
    head_weight = draw_head_weight(jax.random.fold_in(splits[6], 71), 0)
    teacher_logits = draw_teacher_logits(jax.random.fold_in(splits[6], 71), 0)
    block_coeff = draw_block_coeff(jax.random.fold_in(splits[6], 71), 0)
    block_map = draw_block_map(jax.random.fold_in(splits[6], 71), 0)
    return {"hidden": hidden, "token_weight": token_weight, "head_weight": head_weight, "teacher_logits": teacher_logits, "block_coeff": block_coeff, "block_map": block_map}


def teacher_targets(logit_rows, block_coeff, block_map):
    teacher_rows = logit_rows.astype(jnp.float32)
    row_max = jnp.max(teacher_rows, axis=1, keepdims=True)
    row_total = jnp.sum(jnp.exp(teacher_rows - row_max), axis=1, keepdims=True)
    teacher_prob = (jnp.exp(teacher_rows - row_max) / row_total).astype(jnp.bfloat16)
    block_prob = teacher_prob.reshape(teacher_rows.shape[0], TVB, BLK).astype(jnp.float32)
    mapped = jnp.einsum("rbi,bij->brj", block_prob, block_coeff.astype(jnp.float32), precision=lax.Precision.HIGHEST)
    mapped = lax.optimization_barrier(mapped.astype(jnp.bfloat16)).astype(jnp.float32)
    summed = jax.ops.segment_sum(mapped, block_map, num_segments=VS // BLK)
    target = summed.astype(jnp.bfloat16)
    return jnp.transpose(target, (1, 0, 2)).reshape(teacher_rows.shape[0], VS)


def reference(hidden, token_weight, head_weight, teacher_logits, block_coeff, block_map):
    def half_step(grad_weight, block_index):
        device_row = block_index // 2
        fold_side = block_index % 2
        seq_block = jnp.where(fold_side == 0, device_row, 2 * N_CTX - 1 - device_row).astype(jnp.int32)
        hidden_rows = lax.dynamic_slice_in_dim(hidden, block_index * HALF, HALF, 0)
        row_weights = lax.dynamic_slice_in_dim(token_weight, block_index * HALF, HALF, 0).astype(jnp.float32)
        teacher_rows = lax.dynamic_slice_in_dim(teacher_logits, seq_block * HALF, HALF, 0)
        target_full = teacher_targets(teacher_rows, block_coeff, block_map).astype(jnp.float32)
        logits = jnp.dot(hidden_rows, head_weight, preferred_element_type=jnp.float32)
        row_max = jnp.max(logits, axis=1)
        row_total = jnp.sum(jnp.exp(logits - row_max[:, None]), axis=1)
        norm_log = row_max + jnp.log(row_total)
        row_mass = jnp.sum(target_full, axis=1)
        row_cross = jnp.sum(target_full * logits, axis=1)
        row_loss = row_mass * norm_log - row_cross
        grad_logits = (row_weights[:, None] * (row_mass[:, None] * jnp.exp(logits - norm_log[:, None]) - target_full)).astype(jnp.bfloat16)
        grad_rows = lax.dot_general(grad_logits, head_weight, (((1,), (1,)), ((), ())), preferred_element_type=jnp.float32).astype(jnp.bfloat16)
        grad_weight = grad_weight + lax.dot_general(hidden_rows, grad_logits, (((0,), (0,)), ((), ())), preferred_element_type=jnp.float32)
        return grad_weight, (grad_rows, row_loss)

    initial = jnp.zeros((D, VS), jnp.float32)
    grad_weight, (grad_rows, row_loss) = lax.scan(half_step, initial, jnp.arange(2 * N_CTX, dtype=jnp.int32))
    return grad_rows.reshape(TOKENS, D), grad_weight, row_loss.reshape(TOKENS)
```

```python
import functools

import jax
import jax.numpy as jnp
from jax import lax
from jax.experimental import pallas as pl
from jax.experimental.pallas import tpu as pltpu
from jax.sharding import PartitionSpec as P

F32 = jnp.float32
BF16 = jnp.bfloat16
LANES = 128
VMEM_LIMIT = 56 * 1024 * 1024


def params():
    return pltpu.CompilerParams(vmem_limit_bytes=VMEM_LIMIT)


def pieces(value):
    high = value.astype(BF16).astype(F32)
    rest = value - high
    middle = rest.astype(BF16).astype(F32)
    return high, middle, rest - middle


def lanes_of(columns, rows):
    lane = lax.broadcasted_iota(jnp.int32, (rows, LANES), 1)
    tile = jnp.zeros((rows, LANES), F32)
    for index, column in enumerate(columns):
        tile = jnp.where(lane == index, column, tile)
    return tile


def teacher_kernel(logits_ref, coeff_ref, out_ref):
    rows = logits_ref.shape[0]
    groups, _, part, _ = out_ref.shape
    blocks = coeff_ref.shape[0]

    def top(b, carry):
        return jnp.maximum(carry, logits_ref[:, pl.ds(pl.multiple_of(b * LANES, LANES), LANES)])

    widest = lax.fori_loop(
        1, blocks, top, logits_ref[:, 0:LANES], unroll=4
    ).astype(F32)
    row_max = jnp.max(widest, axis=1, keepdims=True)

    def one(b, total):
        x = logits_ref[:, pl.ds(pl.multiple_of(b * LANES, LANES), LANES)].astype(F32)
        e = jnp.exp(x - row_max)
        mapped = jnp.dot(e.astype(BF16), coeff_ref[b], preferred_element_type=F32).astype(BF16)
        out_ref[:, b] = mapped.reshape(groups, part, LANES)
        return total + e

    total = lax.fori_loop(0, blocks, one, jnp.zeros((rows, LANES), F32), unroll=4)
    row_total = jnp.sum(total, axis=1, keepdims=True)
    tile = lanes_of((row_max,) + pieces(row_total), rows).astype(BF16)
    out_ref[:, blocks] = tile.reshape(groups, part, LANES)


def collect_kernel(slot_ref, in_ref, out_ref, mass_ref, sums, scales):
    voc_count, held, part, _ = in_ref.shape
    blocks = held - 1
    slots = out_ref.shape[0]
    tops, totals = [], []
    for v in range(voc_count):
        tile = in_ref[v, blocks].astype(F32)
        tops.append(tile[:, 0:1])
        totals.append(tile[:, 1:2] + tile[:, 2:3] + tile[:, 3:4])
    top = functools.reduce(jnp.maximum, tops)
    total = functools.reduce(
        jnp.add, [part_total * jnp.exp(part_top - top) for part_total, part_top in zip(totals, tops)]
    )
    for v in range(voc_count):
        scales[v] = jnp.broadcast_to(jnp.exp(tops[v] - top) / total, (part, LANES))

    def clear(s, carry):
        sums[s] = jnp.zeros((part, LANES), F32)
        return carry

    lax.fori_loop(0, slots, clear, 0, unroll=8)
    for v in range(voc_count):
        scale = scales[v]

        def add(b, carry):
            slot = slot_ref[v * blocks + b]
            sums[slot] = sums[slot] + scale * in_ref[v, b].astype(F32)
            return carry

        lax.fori_loop(0, blocks, add, 0, unroll=4)

    def store(s, mass):
        target = sums[s].astype(BF16)
        out_ref[s] = target
        return mass + target.astype(F32)

    mass = lax.fori_loop(0, slots, store, jnp.zeros((part, LANES), F32), unroll=8)
    mass_ref[...] = jnp.broadcast_to(jnp.sum(mass, axis=1, keepdims=True), (part, LANES))


def logits_kernel(hidden_ref, weight_ref, mass_ref, logits_ref, stats_ref, tops, totals):
    step = pl.program_id(0)
    rows, cols = logits_ref.shape[1:]

    @pl.when(step == 0)
    def _():
        tops[...] = jnp.full(tops.shape, -jnp.inf, F32)
        totals[...] = jnp.zeros(totals.shape, F32)

    logits = jnp.dot(hidden_ref[...], weight_ref[0], preferred_element_type=F32)
    logits_ref[0] = logits
    tiles = [logits[:, k : k + LANES] for k in range(0, cols, LANES)]
    old = tops[...]
    new = functools.reduce(jnp.maximum, tiles, old)
    total = totals[...] * jnp.exp(old - new)
    for tile in tiles:
        total = total + jnp.exp(tile - new)
    tops[...] = new
    totals[...] = total

    @pl.when(step == pl.num_programs(0) - 1)
    def _():
        lane_top, lane_total = tops[...], totals[...]
        top = jnp.max(lane_top, axis=1, keepdims=True)
        total = jnp.sum(lane_total * jnp.exp(lane_top - top), axis=1, keepdims=True)
        part = mass_ref.shape[0]
        flat = jnp.transpose(lanes_of((top, total), rows))
        mass = jnp.transpose(mass_ref[...])
        mass = jnp.concatenate([mass[0:1], jnp.zeros((1, rows - part), F32)], axis=1)
        packed = jnp.concatenate([flat[0:2], mass, jnp.zeros((1, rows), F32)], axis=0)
        stats_ref[...] = jnp.broadcast_to(packed[None], stats_ref.shape)


def grad_kernel(
    place_ref, stats_ref, logits_ref, target_ref, hidden_ref, hidden_t_ref, weight_ref,
    dweight_ref, dhidden_ref, base_ref, norm, mass, gain, cross, partial,
):
    step = pl.program_id(0)
    count, _, part, _ = target_ref.shape
    rows, cols = logits_ref.shape[1:]
    width = weight_ref.shape[1]

    @pl.when(step == 0)
    def _():
        tops = stats_ref[:, 0, :]
        top = jnp.max(tops, axis=0, keepdims=True)
        total = jnp.sum(stats_ref[:, 1, :] * jnp.exp(tops - top), axis=0, keepdims=True)
        norm_row = jnp.broadcast_to(top + jnp.log(total), (LANES, rows))
        norm[...] = jnp.transpose(norm_row)
        own = stats_ref[:, 2, 0:LANES]
        spread = jnp.broadcast_to(own[:, None, :], (count, part, LANES))
        diagonal = lax.broadcasted_iota(jnp.int32, (count, part, LANES), 1) == lax.broadcasted_iota(
            jnp.int32, (count, part, LANES), 2
        )
        column = jnp.sum(jnp.where(diagonal, spread, 0.0), axis=2, keepdims=True).reshape(rows, 1)
        mass[...] = jnp.broadcast_to(column, (rows, LANES))
        gain[...] = jnp.broadcast_to(
            hidden_ref[:, width : width + LANES].astype(F32)[:, 0:1], (rows, LANES)
        )
        cross[...] = jnp.zeros(cross.shape, F32)

    norm_tile, mass_tile, gain_tile = norm[...], mass[...], gain[...]
    crossed = cross[...]
    grads = []
    for q in range(cols // LANES):
        logit = logits_ref[0, :, q * LANES : (q + 1) * LANES]
        target = target_ref[:, q].reshape(rows, LANES).astype(F32)
        crossed = crossed + target * logit
        grads.append(
            (gain_tile * (mass_tile * jnp.exp(logit - norm_tile) - target)).astype(BF16)
        )
    cross[...] = crossed
    grad = jnp.concatenate(grads, axis=1)
    dweight_ref[0] = jnp.dot(hidden_t_ref[...], grad, preferred_element_type=F32).astype(BF16)
    product = lax.dot_general(
        grad, weight_ref[0], (((1,), (1,)), ((), ())), preferred_element_type=F32
    )

    @pl.when(step == 0)
    def _():
        partial[...] = product

    @pl.when(step > 0)
    def _():
        partial[...] = partial[...] + product

    @pl.when(step == pl.num_programs(0) - 1)
    def _():
        cross_sum = jnp.sum(cross[...], axis=1, keepdims=True)
        cross[...] = lanes_of(pieces(cross_sum), rows)
        for t in range(count):
            c = place_ref[t]
            dhidden_ref[c, :, 0:width] = partial[t * part : (t + 1) * part, :].astype(BF16)
            dhidden_ref[c, :, width : width + LANES] = cross[t * part : (t + 1) * part, :].astype(BF16)
        mass[...] = mass[...] * norm[...]
        start = pl.multiple_of(place_ref[count] * part, part)
        base_ref[...] = mass[pl.ds(start, part), :]


def finish_kernel(in_ref, base_ref, out_ref):
    count, part, wide = in_ref.shape
    width = wide - LANES
    total = jnp.zeros((part, wide), F32)
    for c in range(count):
        total = total + in_ref[c].astype(F32)
    out_ref[:, 0:width] = total[:, 0:width].astype(BF16)
    tail = total[:, width:wide]
    crossed = tail[:, 0:1] + tail[:, 1:2] + tail[:, 2:3]
    loss = base_ref[...][:, 0:1] - crossed
    out_ref[:, width:wide] = lanes_of(pieces(loss), part).astype(BF16)


def whole(shape):
    return pl.BlockSpec(shape, lambda *_: (0,) * len(shape))


def local(hidden, token_weight, head_weight, teacher_logits, block_coeff, block_map):
    ctx_count = lax.axis_size("ctx")
    voc_count = lax.axis_size("voc")
    voc_index = lax.axis_index("voc")
    ctx_index = lax.axis_index("ctx")
    rows_dev, width = hidden.shape
    half_rows = rows_dev // 2
    part = rows_dev // voc_count
    half_groups = voc_count // 2
    local_blocks = block_coeff.shape[0]
    cols = head_weight.shape[1]
    dev_blocks = cols // LANES
    owned_blocks = voc_count * dev_blocks
    slots = ctx_count * owned_blocks
    rows = ctx_count * part
    smem = pl.BlockSpec(memory_space=pltpu.SMEM)

    parity = voc_index // half_groups
    fold = jnp.where(ctx_index % 2 == parity, 0, 1)
    start = fold * half_rows + voc_index % half_groups * part
    mine = lax.dynamic_slice_in_dim(hidden, start, part, 0)
    mine_weight = lax.dynamic_slice_in_dim(token_weight, start, part, 0)
    mine = jnp.concatenate([mine, jnp.broadcast_to(mine_weight[:, None], (part, LANES))], axis=1)
    by_ctx = lax.all_to_all(
        jnp.broadcast_to(mine[None], (ctx_count, part, width + LANES)), "ctx", 0, 0, tiled=True
    )
    source = jnp.arange(ctx_count, dtype=jnp.int32)
    half_block = 2 * source + parity
    place = jnp.where(half_block < ctx_count, half_block, 2 * ctx_count - 1 - half_block)
    own_half = jnp.where(fold == 0, ctx_index, 2 * ctx_count - 1 - ctx_index)
    place = jnp.concatenate([place, (own_half // 2)[None]]).astype(jnp.int32)
    hidden_rows = by_ctx[place[:ctx_count]].reshape(rows, width + LANES)
    hidden_t = hidden_rows[:, :width].T

    outgoing = pl.pallas_call(
        teacher_kernel,
        out_shape=jax.ShapeDtypeStruct((voc_count, local_blocks + 1, part, LANES), BF16),
        compiler_params=params(),
        cost_estimate=pl.CostEstimate(
            flops=2 * rows_dev * local_blocks * LANES * LANES,
            bytes_accessed=6 * 1024 * 1024,
            transcendentals=rows_dev * local_blocks * LANES,
        ),
        name="teacher_map",
    )(teacher_logits, block_coeff)
    incoming = lax.all_to_all(outgoing, "voc", 0, 0, tiled=True)

    head_weight, incoming = lax.optimization_barrier((head_weight, incoming))
    weights = lax.all_gather(head_weight, "voc", axis=0, tiled=False)

    target, mass = pl.pallas_call(
        collect_kernel,
        out_shape=(
            jax.ShapeDtypeStruct((slots, part, LANES), BF16),
            jax.ShapeDtypeStruct((part, LANES), F32),
        ),
        in_specs=[smem, pl.BlockSpec(memory_space=pltpu.VMEM)],
        scratch_shapes=[
            pltpu.VMEM((slots, part, LANES), F32),
            pltpu.VMEM((voc_count, part, LANES), F32),
        ],
        compiler_params=params(),
        cost_estimate=pl.CostEstimate(
            flops=4 * slots * part * LANES, bytes_accessed=6 * 1024 * 1024, transcendentals=0
        ),
        name="collect_targets",
    )(block_map, incoming)
    target = target.reshape(ctx_count, owned_blocks, part, LANES)
    arrived = lax.all_to_all(target, "ctx", 0, 0, tiled=True)

    logits, stats = pl.pallas_call(
        logits_kernel,
        grid=(voc_count,),
        in_specs=[
            pl.BlockSpec((rows, width), lambda j: (0, 0)),
            pl.BlockSpec((1, width, cols), lambda j: (j, 0, 0)),
            whole((part, LANES)),
        ],
        out_specs=(
            pl.BlockSpec((1, rows, cols), lambda j: (j, 0, 0)),
            whole((ctx_count, 4, rows)),
        ),
        out_shape=(
            jax.ShapeDtypeStruct((voc_count, rows, cols), F32),
            jax.ShapeDtypeStruct((ctx_count, 4, rows), F32),
        ),
        scratch_shapes=[pltpu.VMEM((rows, LANES), F32)] * 2,
        compiler_params=params(),
        cost_estimate=pl.CostEstimate(
            flops=2 * rows * width * cols * voc_count,
            bytes_accessed=18 * 1024 * 1024,
            transcendentals=rows * cols * voc_count,
        ),
        name="student_logits",
    )(hidden_rows, weights, mass)
    all_stats = lax.all_to_all(stats, "ctx", 0, 0, tiled=True)

    dweight, dhidden, base = pl.pallas_call(
        grad_kernel,
        grid=(voc_count,),
        in_specs=[
            smem,
            whole((ctx_count, 4, rows)),
            pl.BlockSpec((1, rows, cols), lambda j: (j, 0, 0)),
            pl.BlockSpec((ctx_count, dev_blocks, part, LANES), lambda j: (0, j, 0, 0)),
            whole((rows, width + LANES)),
            whole((width, rows)),
            pl.BlockSpec((1, width, cols), lambda j: (j, 0, 0)),
        ],
        out_specs=(
            pl.BlockSpec((1, width, cols), lambda j: (j, 0, 0)),
            whole((ctx_count, part, width + LANES)),
            whole((part, LANES)),
        ),
        out_shape=(
            jax.ShapeDtypeStruct((voc_count, width, cols), BF16),
            jax.ShapeDtypeStruct((ctx_count, part, width + LANES), BF16),
            jax.ShapeDtypeStruct((part, LANES), F32),
        ),
        scratch_shapes=[pltpu.VMEM((rows, LANES), F32)] * 4 + [pltpu.VMEM((rows, width), F32)],
        compiler_params=params(),
        cost_estimate=pl.CostEstimate(
            flops=4 * rows * width * cols * voc_count,
            bytes_accessed=30 * 1024 * 1024,
            transcendentals=rows * cols * voc_count,
        ),
        name="grads",
    )(place, all_stats, logits, arrived, hidden_rows, hidden_t, weights)
    grad_weight = lax.psum_scatter(dweight, "voc", scatter_dimension=0, tiled=True)
    grad_weight = grad_weight.reshape(width, cols).astype(F32)
    returned = lax.all_to_all(dhidden, "ctx", 0, 0, tiled=True)
    done = pl.pallas_call(
        finish_kernel,
        out_shape=jax.ShapeDtypeStruct((part, width + LANES), BF16),
        compiler_params=params(),
        name="finish_rows",
    )(returned, base)
    all_done = lax.all_gather(done, "voc", axis=0, tiled=False)
    all_done = jnp.where(ctx_index % 2 == 0, all_done, jnp.roll(all_done, half_groups, axis=0))
    all_done = all_done.reshape(rows_dev, width + LANES)
    grad_hidden = all_done[:, :width]
    row_loss = jnp.sum(all_done[:, width : width + 3].astype(F32), axis=1)
    return (grad_hidden, grad_weight, row_loss)


def solution(mesh):
    return jax.shard_map(
        local,
        mesh=mesh,
        in_specs=(
            P("ctx", None),
            P("ctx"),
            P(None, ("ctx", "voc")),
            P("ctx", "voc"),
            P("voc", None, None),
            P(),
        ),
        out_specs=(P("ctx", None), P(None, ("ctx", "voc")), P("ctx")),
        check_vma=False,
    )
```

```python
import functools

import jax
import jax.numpy as jnp
from jax import lax
from jax.experimental import pallas as pl
from jax.experimental.pallas import tpu as pltpu
from jax.sharding import PartitionSpec as P

F32 = jnp.float32
BF16 = jnp.bfloat16
LANES = 128
VMEM_LIMIT = 56 * 1024 * 1024


def params():
    return pltpu.CompilerParams(vmem_limit_bytes=VMEM_LIMIT)


def pieces(value):
    high = value.astype(BF16).astype(F32)
    rest = value - high
    middle = rest.astype(BF16).astype(F32)
    return high, middle, rest - middle


def lanes_of(columns, rows):
    lane = lax.broadcasted_iota(jnp.int32, (rows, LANES), 1)
    tile = jnp.zeros((rows, LANES), F32)
    for index, column in enumerate(columns):
        tile = jnp.where(lane == index, column, tile)
    return tile


def teacher_kernel(logits_ref, coeff_ref, out_ref):
    rows = logits_ref.shape[0]
    groups, _, part, _ = out_ref.shape
    blocks = coeff_ref.shape[0]

    def top(b, carry):
        return jnp.maximum(carry, logits_ref[:, pl.ds(pl.multiple_of(b * LANES, LANES), LANES)])

    widest = lax.fori_loop(
        1, blocks, top, logits_ref[:, 0:LANES], unroll=4
    ).astype(F32)
    row_max = jnp.max(widest, axis=1, keepdims=True)

    def one(b, total):
        x = logits_ref[:, pl.ds(pl.multiple_of(b * LANES, LANES), LANES)].astype(F32)
        e = jnp.exp(x - row_max)
        mapped = jnp.dot(e.astype(BF16), coeff_ref[b], preferred_element_type=F32).astype(BF16)
        out_ref[:, b] = mapped.reshape(groups, part, LANES)
        return total + e

    total = lax.fori_loop(0, blocks, one, jnp.zeros((rows, LANES), F32), unroll=4)
    row_total = jnp.sum(total, axis=1, keepdims=True)
    tile = lanes_of((row_max,) + pieces(row_total), rows).astype(BF16)
    out_ref[:, blocks] = tile.reshape(groups, part, LANES)


def collect_kernel(slot_ref, in_ref, out_ref, sums, scales):
    voc_count, held, part, _ = in_ref.shape
    blocks = held - 1
    ctx_count, owned = out_ref.shape[0], out_ref.shape[1] - 1
    slots = ctx_count * owned
    tops, totals = [], []
    for v in range(voc_count):
        tile = in_ref[v, blocks].astype(F32)
        tops.append(tile[:, 0:1])
        totals.append(tile[:, 1:2] + tile[:, 2:3] + tile[:, 3:4])
    top = functools.reduce(jnp.maximum, tops)
    total = functools.reduce(
        jnp.add, [part_total * jnp.exp(part_top - top) for part_total, part_top in zip(totals, tops)]
    )
    for v in range(voc_count):
        scales[v] = jnp.broadcast_to(jnp.exp(tops[v] - top) / total, (part, LANES))

    def clear(s, carry):
        sums[s] = jnp.zeros((part, LANES), F32)
        return carry

    lax.fori_loop(0, slots, clear, 0, unroll=8)
    for v in range(voc_count):
        scale = scales[v]

        def add(b, carry):
            slot = slot_ref[v * blocks + b]
            sums[slot] = sums[slot] + scale * in_ref[v, b].astype(F32)
            return carry

        lax.fori_loop(0, blocks, add, 0, unroll=4)

    def store(c, mass):
        for k in range(owned):
            target = sums[c * owned + k].astype(BF16)
            out_ref[c, k] = target
            mass = mass + target.astype(F32)
        return mass

    mass = lax.fori_loop(0, ctx_count, store, jnp.zeros((part, LANES), F32))
    tile = lanes_of(pieces(jnp.sum(mass, axis=1, keepdims=True)), part).astype(BF16)
    for c in range(ctx_count):
        out_ref[c, owned] = tile


def logits_kernel(hidden_ref, weight_ref, logits_ref, stats_ref, tops, totals):
    step = pl.program_id(0)
    rows, cols = logits_ref.shape[1:]

    @pl.when(step == 0)
    def _():
        tops[...] = jnp.full(tops.shape, -jnp.inf, F32)
        totals[...] = jnp.zeros(totals.shape, F32)

    logits = jnp.dot(hidden_ref[...], weight_ref[0], preferred_element_type=F32)
    logits_ref[0] = logits
    tiles = [logits[:, k : k + LANES] for k in range(0, cols, LANES)]
    old = tops[...]
    new = functools.reduce(jnp.maximum, tiles, old)
    total = totals[...] * jnp.exp(old - new)
    for tile in tiles:
        total = total + jnp.exp(tile - new)
    tops[...] = new
    totals[...] = total

    @pl.when(step == pl.num_programs(0) - 1)
    def _():
        lane_top, lane_total = tops[...], totals[...]
        top = jnp.max(lane_top, axis=1, keepdims=True)
        total = jnp.sum(lane_total * jnp.exp(lane_top - top), axis=1, keepdims=True)
        stats_ref[...] = jnp.transpose(lanes_of((top, total), rows))[0 : stats_ref.shape[0]]


def grad_kernel(
    place_ref, stats_ref, mass_ref, logits_ref, target_ref, hidden_ref, hidden_t_ref, weight_ref,
    dweight_ref, dhidden_ref, base_ref, norm, mass, gain, cross, partial,
):
    step = pl.program_id(0)
    count, _, part, _ = target_ref.shape
    rows, cols = logits_ref.shape[1:]
    width = weight_ref.shape[1]

    @pl.when(step == 0)
    def _():
        top, total = stats_ref[0:1], stats_ref[1:2]
        norm[...] = jnp.transpose(jnp.broadcast_to(top + jnp.log(total), (LANES, rows)))
        sent = mass_ref[...].reshape(rows, LANES).astype(F32)
        mass[...] = jnp.broadcast_to(sent[:, 0:1] + sent[:, 1:2] + sent[:, 2:3], (rows, LANES))
        gain[...] = jnp.broadcast_to(
            hidden_ref[:, width : width + LANES].astype(F32)[:, 0:1], (rows, LANES)
        )
        cross[...] = jnp.zeros(cross.shape, F32)

    norm_tile, mass_tile, gain_tile = norm[...], mass[...], gain[...]
    crossed = cross[...]
    grads = []
    for q in range(cols // LANES):
        logit = logits_ref[0, :, q * LANES : (q + 1) * LANES]
        target = target_ref[:, q].reshape(rows, LANES).astype(F32)
        crossed = crossed + target * logit
        grads.append(
            (gain_tile * (mass_tile * jnp.exp(logit - norm_tile) - target)).astype(BF16)
        )
    cross[...] = crossed
    grad = jnp.concatenate(grads, axis=1)
    dweight_ref[0] = jnp.dot(hidden_t_ref[...], grad, preferred_element_type=F32).astype(BF16)
    product = lax.dot_general(
        grad, weight_ref[0], (((1,), (1,)), ((), ())), preferred_element_type=F32
    )

    @pl.when(step == 0)
    def _():
        partial[...] = product

    @pl.when(step > 0)
    def _():
        partial[...] = partial[...] + product

    @pl.when(step == pl.num_programs(0) - 1)
    def _():
        cross_sum = jnp.sum(cross[...], axis=1, keepdims=True)
        cross[...] = lanes_of(pieces(cross_sum), rows)
        for t in range(count):
            c = place_ref[t]
            dhidden_ref[c, :, 0:width] = partial[t * part : (t + 1) * part, :].astype(BF16)
            dhidden_ref[c, :, width : width + LANES] = cross[t * part : (t + 1) * part, :].astype(BF16)
        mass[...] = mass[...] * norm[...]
        start = pl.multiple_of(place_ref[count] * part, part)
        base_ref[...] = mass[pl.ds(start, part), :]


def fold(refs):
    wide = refs[0].shape[-1]
    total = refs[0][...].astype(F32)
    for ref in refs[1:]:
        total = total + ref[...].astype(F32)
    tail = total[:, wide - LANES :]
    return total[:, : wide - LANES], tail[:, 0:1] + tail[:, 1:2] + tail[:, 2:3]


def fold_kernel(*refs):
    out_ref = refs[-1]
    rows, wide = out_ref.shape
    total, crossed = fold(refs[:-1])
    out_ref[:, 0 : wide - LANES] = total.astype(BF16)
    out_ref[:, wide - LANES : wide] = lanes_of(pieces(crossed), rows).astype(BF16)


def finish_kernel(*refs):
    base_ref, out_ref = refs[-2:]
    rows, wide = out_ref.shape
    total, crossed = fold(refs[:-2])
    out_ref[:, 0 : wide - LANES] = total.astype(BF16)
    loss = base_ref[:, 0:1] - crossed
    out_ref[:, wide - LANES : wide] = lanes_of(pieces(loss), rows).astype(BF16)


def whole(shape):
    return pl.BlockSpec(shape, lambda *_: (0,) * len(shape))


def shifted(value, ring, along_x, step):
    count = lax.axis_size("ctx")
    lines = count // ring
    pairs = []
    for x in range(lines):
        for z in range(ring):
            to = (x + step) % lines * ring + z if along_x else x * ring + (z + step) % ring
            pairs.append((x * ring + z, to))
    return lax.ppermute(value, "ctx", pairs)


def spread(value, ring, along_x):
    count = lax.axis_size("ctx") // ring if along_x else ring
    return [value] + [shifted(value, ring, along_x, step) for step in range(1, count)]


def merged(stats):
    top = functools.reduce(jnp.maximum, [part[0:1] for part in stats])
    total = functools.reduce(jnp.add, [part[1:2] * jnp.exp(part[0:1] - top) for part in stats])
    return jnp.concatenate([top, total], axis=0)


def local(hidden, token_weight, head_weight, teacher_logits, block_coeff, block_map):
    ctx_count = lax.axis_size("ctx")
    voc_count = lax.axis_size("voc")
    voc_index = lax.axis_index("voc")
    ctx_index = lax.axis_index("ctx")
    rows_dev, width = hidden.shape
    half_rows = rows_dev // 2
    part = rows_dev // voc_count
    half_groups = voc_count // 2
    local_blocks = block_coeff.shape[0]
    cols = head_weight.shape[1]
    dev_blocks = cols // LANES
    owned_blocks = voc_count * dev_blocks
    slots = ctx_count * owned_blocks
    rows = ctx_count * part
    smem = pl.BlockSpec(memory_space=pltpu.SMEM)

    parity = voc_index // half_groups
    fold_side = jnp.where(ctx_index % 2 == parity, 0, 1)
    start = fold_side * half_rows + voc_index % half_groups * part
    mine = lax.dynamic_slice_in_dim(hidden, start, part, 0)
    mine_weight = lax.dynamic_slice_in_dim(token_weight, start, part, 0)
    mine = jnp.concatenate([mine, jnp.broadcast_to(mine_weight[:, None], (part, LANES))], axis=1)
    ring = min(8, ctx_count)
    near = jnp.stack(spread(mine, ring, False))
    by_ctx = jnp.concatenate(spread(near, ring, True), axis=0)
    source = jnp.arange(ctx_count, dtype=jnp.int32)
    half_block = 2 * source + parity
    place = jnp.where(half_block < ctx_count, half_block, 2 * ctx_count - 1 - half_block)
    own_half = jnp.where(fold_side == 0, ctx_index, 2 * ctx_count - 1 - ctx_index)
    behind = (ctx_index // ring - place // ring) % (ctx_count // ring) * ring + (ctx_index - place) % ring
    ahead = (place // ring - ctx_index // ring) % (ctx_count // ring) * ring + (place - ctx_index) % ring
    place = jnp.concatenate([ahead, (own_half // 2)[None]]).astype(jnp.int32)
    hidden_rows = by_ctx[behind].reshape(rows, width + LANES)
    hidden_t = hidden_rows[:, :width].T

    outgoing = pl.pallas_call(
        teacher_kernel,
        out_shape=jax.ShapeDtypeStruct((voc_count, local_blocks + 1, part, LANES), BF16),
        compiler_params=params(),
        cost_estimate=pl.CostEstimate(
            flops=2 * rows_dev * local_blocks * LANES * LANES,
            bytes_accessed=6 * 1024 * 1024,
            transcendentals=rows_dev * local_blocks * LANES,
        ),
        name="teacher_map",
    )(teacher_logits, block_coeff)
    incoming = lax.all_to_all(outgoing, "voc", 0, 0, tiled=True)

    head_weight, incoming = lax.optimization_barrier((head_weight, incoming))
    weights = lax.all_gather(head_weight, "voc", axis=0, tiled=False)

    target = pl.pallas_call(
        collect_kernel,
        out_shape=jax.ShapeDtypeStruct((ctx_count, owned_blocks + 1, part, LANES), BF16),
        in_specs=[smem, pl.BlockSpec(memory_space=pltpu.VMEM)],
        scratch_shapes=[
            pltpu.VMEM((slots, part, LANES), F32),
            pltpu.VMEM((voc_count, part, LANES), F32),
        ],
        compiler_params=params(),
        cost_estimate=pl.CostEstimate(
            flops=4 * slots * part * LANES, bytes_accessed=6 * 1024 * 1024, transcendentals=0
        ),
        name="collect_targets",
    )(block_map, incoming)
    arrived = lax.all_to_all(target, "ctx", 0, 0, tiled=True)

    logits, stats = pl.pallas_call(
        logits_kernel,
        grid=(voc_count,),
        in_specs=[
            pl.BlockSpec((rows, width), lambda j: (0, 0)),
            pl.BlockSpec((1, width, cols), lambda j: (j, 0, 0)),
        ],
        out_specs=(
            pl.BlockSpec((1, rows, cols), lambda j: (j, 0, 0)),
            whole((8, rows)),
        ),
        out_shape=(
            jax.ShapeDtypeStruct((voc_count, rows, cols), F32),
            jax.ShapeDtypeStruct((8, rows), F32),
        ),
        scratch_shapes=[pltpu.VMEM((rows, LANES), F32)] * 2,
        compiler_params=params(),
        cost_estimate=pl.CostEstimate(
            flops=2 * rows * width * cols * voc_count,
            bytes_accessed=18 * 1024 * 1024,
            transcendentals=rows * cols * voc_count,
        ),
        name="student_logits",
    )(hidden_rows, weights)
    stats = merged(spread(stats, ring, False))
    stats = merged(spread(stats, ring, True))

    dweight, dhidden, base = pl.pallas_call(
        grad_kernel,
        grid=(voc_count,),
        in_specs=[
            smem,
            whole((2, rows)),
            pl.BlockSpec((ctx_count, 1, part, LANES), lambda j: (0, owned_blocks, 0, 0)),
            pl.BlockSpec((1, rows, cols), lambda j: (j, 0, 0)),
            pl.BlockSpec((ctx_count, dev_blocks, part, LANES), lambda j: (0, j, 0, 0)),
            whole((rows, width + LANES)),
            whole((width, rows)),
            pl.BlockSpec((1, width, cols), lambda j: (j, 0, 0)),
        ],
        out_specs=(
            pl.BlockSpec((1, width, cols), lambda j: (j, 0, 0)),
            whole((ctx_count, part, width + LANES)),
            whole((part, LANES)),
        ),
        out_shape=(
            jax.ShapeDtypeStruct((voc_count, width, cols), BF16),
            jax.ShapeDtypeStruct((ctx_count, part, width + LANES), BF16),
            jax.ShapeDtypeStruct((part, LANES), F32),
        ),
        scratch_shapes=[pltpu.VMEM((rows, LANES), F32)] * 4 + [pltpu.VMEM((rows, width), F32)],
        compiler_params=params(),
        cost_estimate=pl.CostEstimate(
            flops=4 * rows * width * cols * voc_count,
            bytes_accessed=30 * 1024 * 1024,
            transcendentals=rows * cols * voc_count,
        ),
        name="grads",
    )(place, stats, arrived, logits, arrived, hidden_rows, hidden_t, weights)
    grad_weight = lax.psum_scatter(dweight, "voc", scatter_dimension=0, tiled=True)
    grad_weight = grad_weight.reshape(width, cols).astype(F32)
    wide = width + LANES
    pieces_x = dhidden.reshape(ctx_count // ring, ring * part, wide)
    parts = [pieces_x[0]]
    parts += [shifted(pieces_x[e], ring, True, e) for e in range(1, ctx_count // ring)]
    folded = pl.pallas_call(
        fold_kernel,
        out_shape=jax.ShapeDtypeStruct((ring * part, wide), BF16),
        compiler_params=params(),
        name="fold_rows",
    )(*parts)
    pieces_z = folded.reshape(ring, part, wide)
    parts = [pieces_z[0]] + [shifted(pieces_z[e], ring, False, e) for e in range(1, ring)]
    done = pl.pallas_call(
        finish_kernel,
        out_shape=jax.ShapeDtypeStruct((part, wide), BF16),
        compiler_params=params(),
        name="finish_rows",
    )(*parts, base)
    all_done = lax.all_gather(done, "voc", axis=0, tiled=False)
    all_done = jnp.where(ctx_index % 2 == 0, all_done, jnp.roll(all_done, half_groups, axis=0))
    all_done = all_done.reshape(rows_dev, width + LANES)
    grad_hidden = all_done[:, :width]
    row_loss = jnp.sum(all_done[:, width : width + 3].astype(F32), axis=1)
    return (grad_hidden, grad_weight, row_loss)


def solution(mesh):
    return jax.shard_map(
        local,
        mesh=mesh,
        in_specs=(
            P("ctx", None),
            P("ctx"),
            P(None, ("ctx", "voc")),
            P("ctx", "voc"),
            P("voc", None, None),
            P(),
        ),
        out_specs=(P("ctx", None), P(None, ("ctx", "voc")), P("ctx")),
        check_vma=False,
    )
```

```python
import functools

import jax
import jax.numpy as jnp
from jax import lax
from jax.experimental import pallas as pl
from jax.experimental.pallas import tpu as pltpu
from jax.sharding import PartitionSpec as P

F32 = jnp.float32
BF16 = jnp.bfloat16
LANES = 128
COMPACT = 20
VMEM_LIMIT = 56 * 1024 * 1024


def params():
    return pltpu.CompilerParams(vmem_limit_bytes=VMEM_LIMIT)


def pieces(value):
    high = value.astype(BF16).astype(F32)
    rest = value - high
    middle = rest.astype(BF16).astype(F32)
    return high, middle, rest - middle


def lanes_of(columns, rows):
    lane = lax.broadcasted_iota(jnp.int32, (rows, LANES), 1)
    tile = jnp.zeros((rows, LANES), F32)
    for index, column in enumerate(columns):
        tile = jnp.where(lane == index, column, tile)
    return tile


def teacher_kernel(logits_ref, coeff_ref, out_ref):
    rows = logits_ref.shape[0]
    groups, _, part, _ = out_ref.shape
    blocks = coeff_ref.shape[0]

    def top(b, carry):
        return jnp.maximum(carry, logits_ref[:, pl.ds(pl.multiple_of(b * LANES, LANES), LANES)])

    widest = lax.fori_loop(
        1, blocks, top, logits_ref[:, 0:LANES], unroll=4
    ).astype(F32)
    row_max = jnp.max(widest, axis=1, keepdims=True)

    def one(b, total):
        x = logits_ref[:, pl.ds(pl.multiple_of(b * LANES, LANES), LANES)].astype(F32)
        e = jnp.exp(x - row_max)
        mapped = jnp.dot(e.astype(BF16), coeff_ref[b], preferred_element_type=F32).astype(BF16)
        out_ref[:, b] = mapped.reshape(groups, part, LANES)
        return total + e

    total = lax.fori_loop(0, blocks, one, jnp.zeros((rows, LANES), F32), unroll=4)
    row_total = jnp.sum(total, axis=1, keepdims=True)
    tile = lanes_of((row_max,) + pieces(row_total), rows).astype(BF16)
    out_ref[:, blocks] = tile.reshape(groups, part, LANES)


def collect_kernel(slot_ref, in_ref, out_ref, mass_ref, sums, scales):
    voc_count, held, part, _ = in_ref.shape
    blocks = held - 1
    slots = out_ref.shape[0]
    tops, totals = [], []
    for v in range(voc_count):
        tile = in_ref[v, blocks].astype(F32)
        tops.append(tile[:, 0:1])
        totals.append(tile[:, 1:2] + tile[:, 2:3] + tile[:, 3:4])
    top = functools.reduce(jnp.maximum, tops)
    total = functools.reduce(
        jnp.add, [part_total * jnp.exp(part_top - top) for part_total, part_top in zip(totals, tops)]
    )
    for v in range(voc_count):
        scales[v] = jnp.broadcast_to(jnp.exp(tops[v] - top) / total, (part, LANES))

    def clear(s, carry):
        sums[s] = jnp.zeros((part, LANES), F32)
        return carry

    lax.fori_loop(0, slots, clear, 0, unroll=8)
    for v in range(voc_count):
        scale = scales[v]

        def add(b, carry):
            slot = slot_ref[v * blocks + b]
            sums[slot] = sums[slot] + scale * in_ref[v, b].astype(F32)
            return carry

        lax.fori_loop(0, blocks, add, 0, unroll=4)

    def store(s, mass):
        target = sums[s].astype(BF16)
        out_ref[s] = target
        return mass + target.astype(F32)

    mass = lax.fori_loop(0, slots, store, jnp.zeros((part, LANES), F32), unroll=8)
    mass_ref[...] = jnp.broadcast_to(jnp.sum(mass, axis=1, keepdims=True), (part, LANES))


def logits_kernel(hidden_ref, weight_ref, mass_ref, logits_ref, stats_ref, tops, totals):
    step = pl.program_id(0)
    rows, cols = logits_ref.shape[1:]

    @pl.when(step == 0)
    def _():
        tops[...] = jnp.full(tops.shape, -jnp.inf, F32)
        totals[...] = jnp.zeros(totals.shape, F32)

    logits = jnp.dot(hidden_ref[...], weight_ref[0], preferred_element_type=F32)
    logits_ref[0] = logits
    tiles = [logits[:, k : k + LANES] for k in range(0, cols, LANES)]
    old = tops[...]
    new = functools.reduce(jnp.maximum, tiles, old)
    total = totals[...] * jnp.exp(old - new)
    for tile in tiles:
        total = total + jnp.exp(tile - new)
    tops[...] = new
    totals[...] = total

    @pl.when(step == pl.num_programs(0) - 1)
    def _():
        lane_top, lane_total = tops[...], totals[...]
        top = jnp.max(lane_top, axis=1, keepdims=True)
        total = jnp.sum(lane_total * jnp.exp(lane_top - top), axis=1, keepdims=True)
        part = mass_ref.shape[0]
        flat = jnp.transpose(lanes_of((top, total), rows))
        mass = jnp.transpose(mass_ref[...])
        mass = jnp.concatenate([mass[0:1], jnp.zeros((1, rows - part), F32)], axis=1)
        packed = jnp.concatenate([flat[0:2], mass, jnp.zeros((1, rows), F32)], axis=0)
        stats_ref[...] = jnp.broadcast_to(packed[None], stats_ref.shape)


def grad_kernel(
    place_ref, slot_ref, stats_ref, logits_ref, target_ref, hidden_ref, hidden_t_ref, weight_ref,
    dweight_ref, dhidden_ref, base_ref, norm, mass, gain, cross, partial,
):
    step = pl.program_id(0)
    count, _, part, _ = target_ref.shape
    rows, cols = logits_ref.shape[1:]
    width = weight_ref.shape[1]

    @pl.when(step == 0)
    def _():
        tops = stats_ref[:, 0, :]
        top = jnp.max(tops, axis=0, keepdims=True)
        total = jnp.sum(stats_ref[:, 1, :] * jnp.exp(tops - top), axis=0, keepdims=True)
        norm_row = jnp.broadcast_to(top + jnp.log(total), (LANES, rows))
        norm[...] = jnp.transpose(norm_row)
        own = stats_ref[:, 2, 0:LANES]
        spread = jnp.broadcast_to(own[:, None, :], (count, part, LANES))
        diagonal = lax.broadcasted_iota(jnp.int32, (count, part, LANES), 1) == lax.broadcasted_iota(
            jnp.int32, (count, part, LANES), 2
        )
        column = jnp.sum(jnp.where(diagonal, spread, 0.0), axis=2, keepdims=True).reshape(rows, 1)
        mass[...] = jnp.broadcast_to(column, (rows, LANES))
        gain[...] = jnp.broadcast_to(
            hidden_ref[:, width : width + LANES].astype(F32)[:, 0:1], (rows, LANES)
        )
        cross[...] = jnp.zeros(cross.shape, F32)

    norm_tile, mass_tile, gain_tile = norm[...], mass[...], gain[...]
    crossed = cross[...]
    grads = []
    for q in range(cols // LANES):
        logit = logits_ref[0, :, q * LANES : (q + 1) * LANES]
        slot = slot_ref[step * (cols // LANES) + q]
        held = target_ref[:, jnp.maximum(slot, 0)].reshape(rows, LANES).astype(F32)
        target = jnp.where(slot >= 0, held, 0.0)
        crossed = crossed + target * logit
        grads.append(
            (gain_tile * (mass_tile * jnp.exp(logit - norm_tile) - target)).astype(BF16)
        )
    cross[...] = crossed
    grad = jnp.concatenate(grads, axis=1)
    dweight_ref[0] = jnp.dot(hidden_t_ref[...], grad, preferred_element_type=F32).astype(BF16)
    product = lax.dot_general(
        grad, weight_ref[0], (((1,), (1,)), ((), ())), preferred_element_type=F32
    )

    @pl.when(step == 0)
    def _():
        partial[...] = product

    @pl.when(step > 0)
    def _():
        partial[...] = partial[...] + product

    @pl.when(step == pl.num_programs(0) - 1)
    def _():
        cross_sum = jnp.sum(cross[...], axis=1, keepdims=True)
        cross[...] = lanes_of(pieces(cross_sum), rows)
        for t in range(count):
            c = place_ref[t]
            dhidden_ref[c, :, 0:width] = partial[t * part : (t + 1) * part, :].astype(BF16)
            dhidden_ref[c, :, width : width + LANES] = cross[t * part : (t + 1) * part, :].astype(BF16)
        mass[...] = mass[...] * norm[...]
        start = pl.multiple_of(place_ref[count] * part, part)
        base_ref[...] = mass[pl.ds(start, part), :]


def fold(refs):
    wide = refs[0].shape[-1]
    total = refs[0][...].astype(F32)
    for ref in refs[1:]:
        total = total + ref[...].astype(F32)
    tail = total[:, wide - LANES :]
    return total[:, : wide - LANES], tail[:, 0:1] + tail[:, 1:2] + tail[:, 2:3]


def fold_kernel(*refs):
    out_ref = refs[-1]
    rows, wide = out_ref.shape
    total, crossed = fold(refs[:-1])
    out_ref[:, 0 : wide - LANES] = total.astype(BF16)
    out_ref[:, wide - LANES : wide] = lanes_of(pieces(crossed), rows).astype(BF16)


def finish_kernel(*refs):
    base_ref, out_ref = refs[-2:]
    rows, wide = out_ref.shape
    total, crossed = fold(refs[:-2])
    out_ref[:, 0 : wide - LANES] = total.astype(BF16)
    loss = base_ref[:, 0:1] - crossed
    out_ref[:, wide - LANES : wide] = lanes_of(pieces(loss), rows).astype(BF16)


def whole(shape):
    return pl.BlockSpec(shape, lambda *_: (0,) * len(shape))


def shifted(value, ring, along_x, step):
    count = lax.axis_size("ctx")
    lines = count // ring
    pairs = []
    for x in range(lines):
        for z in range(ring):
            to = (x + step) % lines * ring + z if along_x else x * ring + (z + step) % ring
            pairs.append((x * ring + z, to))
    return lax.ppermute(value, "ctx", pairs)


def spread(value, ring, along_x):
    count = lax.axis_size("ctx") // ring if along_x else ring
    return [value] + [shifted(value, ring, along_x, step) for step in range(1, count)]


def exchange(
    capacity, head_weight, incoming, compact_slot, whole_slot, own_slot, place, behind, by_ctx
):
    ctx_count = lax.axis_size("ctx")
    voc_count, held, part, _ = incoming.shape
    width, cols = head_weight.shape
    dev_blocks = cols // LANES
    owned_blocks = voc_count * dev_blocks
    rows = ctx_count * part
    slots = ctx_count * capacity
    smem = pl.BlockSpec(memory_space=pltpu.SMEM)

    weights = lax.all_gather(head_weight, "voc", axis=0, tiled=False)
    slot = compact_slot if capacity == COMPACT else whole_slot
    target, mass = pl.pallas_call(
        collect_kernel,
        out_shape=(
            jax.ShapeDtypeStruct((slots, part, LANES), BF16),
            jax.ShapeDtypeStruct((part, LANES), F32),
        ),
        in_specs=[smem, pl.BlockSpec(memory_space=pltpu.VMEM)],
        scratch_shapes=[
            pltpu.VMEM((slots, part, LANES), F32),
            pltpu.VMEM((voc_count, part, LANES), F32),
        ],
        compiler_params=params(),
        cost_estimate=pl.CostEstimate(
            flops=4 * slots * part * LANES, bytes_accessed=6 * 1024 * 1024, transcendentals=0
        ),
        name="collect_targets",
    )(slot, incoming)
    target = target.reshape(ctx_count, capacity, part, LANES)
    arrived = lax.all_to_all(target, "ctx", 0, 0, tiled=True)
    hidden_rows = by_ctx[behind].reshape(rows, width + LANES)
    hidden_t = hidden_rows[:, :width].T

    logits, stats = pl.pallas_call(
        logits_kernel,
        grid=(voc_count,),
        in_specs=[
            pl.BlockSpec((rows, width), lambda j: (0, 0)),
            pl.BlockSpec((1, width, cols), lambda j: (j, 0, 0)),
            whole((part, LANES)),
        ],
        out_specs=(
            pl.BlockSpec((1, rows, cols), lambda j: (j, 0, 0)),
            whole((ctx_count, 4, rows)),
        ),
        out_shape=(
            jax.ShapeDtypeStruct((voc_count, rows, cols), F32),
            jax.ShapeDtypeStruct((ctx_count, 4, rows), F32),
        ),
        scratch_shapes=[pltpu.VMEM((rows, LANES), F32)] * 2,
        compiler_params=params(),
        cost_estimate=pl.CostEstimate(
            flops=2 * rows * width * cols * voc_count,
            bytes_accessed=18 * 1024 * 1024,
            transcendentals=rows * cols * voc_count,
        ),
        name="student_logits",
    )(hidden_rows, weights, mass)
    all_stats = lax.all_to_all(stats, "ctx", 0, 0, tiled=True)

    dweight, dhidden, base = pl.pallas_call(
        grad_kernel,
        grid=(voc_count,),
        in_specs=[
            smem,
            smem,
            whole((ctx_count, 4, rows)),
            pl.BlockSpec((1, rows, cols), lambda j: (j, 0, 0)),
            whole((ctx_count, capacity, part, LANES)),
            whole((rows, width + LANES)),
            whole((width, rows)),
            pl.BlockSpec((1, width, cols), lambda j: (j, 0, 0)),
        ],
        out_specs=(
            pl.BlockSpec((1, width, cols), lambda j: (j, 0, 0)),
            whole((ctx_count, part, width + LANES)),
            whole((part, LANES)),
        ),
        out_shape=(
            jax.ShapeDtypeStruct((voc_count, width, cols), BF16),
            jax.ShapeDtypeStruct((ctx_count, part, width + LANES), BF16),
            jax.ShapeDtypeStruct((part, LANES), F32),
        ),
        scratch_shapes=[pltpu.VMEM((rows, LANES), F32)] * 4 + [pltpu.VMEM((rows, width), F32)],
        compiler_params=params(),
        cost_estimate=pl.CostEstimate(
            flops=4 * rows * width * cols * voc_count,
            bytes_accessed=30 * 1024 * 1024,
            transcendentals=rows * cols * voc_count,
        ),
        name="grads",
    )(place, own_slot, all_stats, logits, arrived, hidden_rows, hidden_t, weights)
    return dweight, dhidden, base


def local(hidden, token_weight, head_weight, teacher_logits, block_coeff, block_map):
    ctx_count = lax.axis_size("ctx")
    voc_count = lax.axis_size("voc")
    voc_index = lax.axis_index("voc")
    ctx_index = lax.axis_index("ctx")
    rows_dev, width = hidden.shape
    half_rows = rows_dev // 2
    part = rows_dev // voc_count
    half_groups = voc_count // 2
    local_blocks = block_coeff.shape[0]
    cols = head_weight.shape[1]
    dev_blocks = cols // LANES
    owned_blocks = voc_count * dev_blocks
    slots = ctx_count * owned_blocks
    rows = ctx_count * part
    wide = width + LANES

    parity = voc_index // half_groups
    fold_side = jnp.where(ctx_index % 2 == parity, 0, 1)
    start = fold_side * half_rows + voc_index % half_groups * part
    mine = lax.dynamic_slice_in_dim(hidden, start, part, 0)
    mine_weight = lax.dynamic_slice_in_dim(token_weight, start, part, 0)
    mine = jnp.concatenate([mine, jnp.broadcast_to(mine_weight[:, None], (part, LANES))], axis=1)
    ring = min(8, ctx_count)
    outgoing = pl.pallas_call(
        teacher_kernel,
        out_shape=jax.ShapeDtypeStruct((voc_count, local_blocks + 1, part, LANES), BF16),
        compiler_params=params(),
        cost_estimate=pl.CostEstimate(
            flops=2 * rows_dev * local_blocks * LANES * LANES,
            bytes_accessed=6 * 1024 * 1024,
            transcendentals=rows_dev * local_blocks * LANES,
        ),
        name="teacher_map",
    )(teacher_logits, block_coeff)
    near = jnp.stack(spread(mine, ring, False))
    incoming = lax.all_to_all(outgoing, "voc", 0, 0, tiled=True)

    wanted = jnp.any(
        block_map[:, None] == jnp.arange(slots, dtype=jnp.int32)[None, :], axis=0
    ).astype(jnp.int32).reshape(ctx_count, owned_blocks)
    number = jnp.cumsum(wanted, axis=1) - wanted
    fits = jnp.max(jnp.sum(wanted, axis=1)) <= COMPACT
    own_slot = jnp.where(wanted == 1, number, -1)
    own_slot = lax.dynamic_index_in_dim(own_slot, ctx_index, 0, keepdims=False)
    in_order = number.reshape(slots)[block_map]
    compact_slot = block_map // owned_blocks * COMPACT + in_order
    whole_slot = block_map // owned_blocks * owned_blocks + in_order

    source = jnp.arange(ctx_count, dtype=jnp.int32)
    half_block = 2 * source + parity
    place = jnp.where(half_block < ctx_count, half_block, 2 * ctx_count - 1 - half_block)
    own_half = jnp.where(fold_side == 0, ctx_index, 2 * ctx_count - 1 - ctx_index)
    behind = (ctx_index // ring - place // ring) % (ctx_count // ring) * ring + (ctx_index - place) % ring
    ahead = (place // ring - ctx_index // ring) % (ctx_count // ring) * ring + (place - ctx_index) % ring
    place = jnp.concatenate([ahead, (own_half // 2)[None]]).astype(jnp.int32)
    by_ctx = jnp.concatenate(spread(near, ring, True), axis=0)
    operands = lax.optimization_barrier(
        (incoming, compact_slot, whole_slot, own_slot, place, behind, by_ctx)
    )
    dweight, dhidden, base = lax.cond(
        fits,
        functools.partial(exchange, COMPACT),
        functools.partial(exchange, owned_blocks),
        head_weight,
        *operands,
    )
    grad_weight = lax.psum_scatter(dweight, "voc", scatter_dimension=0, tiled=True)
    grad_weight = grad_weight.reshape(width, cols).astype(F32)
    pieces_x = dhidden.reshape(ctx_count // ring, ring * part, wide)
    parts = [pieces_x[0]]
    parts += [shifted(pieces_x[e], ring, True, e) for e in range(1, ctx_count // ring)]
    folded = pl.pallas_call(
        fold_kernel,
        out_shape=jax.ShapeDtypeStruct((ring * part, wide), BF16),
        compiler_params=params(),
        name="fold_rows",
    )(*parts)
    pieces_z = folded.reshape(ring, part, wide)
    parts = [pieces_z[0]] + [shifted(pieces_z[e], ring, False, e) for e in range(1, ring)]
    done = pl.pallas_call(
        finish_kernel,
        out_shape=jax.ShapeDtypeStruct((part, wide), BF16),
        compiler_params=params(),
        name="finish_rows",
    )(*parts, base)
    all_done = lax.all_gather(done, "voc", axis=0, tiled=False)
    all_done = jnp.where(ctx_index % 2 == 0, all_done, jnp.roll(all_done, half_groups, axis=0))
    all_done = all_done.reshape(rows_dev, width + LANES)
    grad_hidden = all_done[:, :width]
    row_loss = jnp.sum(all_done[:, width : width + 3].astype(F32), axis=1)
    return (grad_hidden, grad_weight, row_loss)


def solution(mesh):
    return jax.shard_map(
        local,
        mesh=mesh,
        in_specs=(
            P("ctx", None),
            P("ctx"),
            P(None, ("ctx", "voc")),
            P("ctx", "voc"),
            P("voc", None, None),
            P(),
        ),
        out_specs=(P("ctx", None), P(None, ("ctx", "voc")), P("ctx")),
        check_vma=False,
    )
```

```python
import functools

import jax
import jax.numpy as jnp
from jax import lax
from jax.experimental import pallas as pl
from jax.experimental.pallas import tpu as pltpu
from jax.sharding import PartitionSpec as P

F32 = jnp.float32
BF16 = jnp.bfloat16
LANES = 128
COMPACT = 20
VMEM_LIMIT = 56 * 1024 * 1024


def params():
    return pltpu.CompilerParams(vmem_limit_bytes=VMEM_LIMIT)


def pieces(value):
    high = value.astype(BF16).astype(F32)
    rest = value - high
    middle = rest.astype(BF16).astype(F32)
    return high, middle, rest - middle


def lanes_of(columns, rows):
    lane = lax.broadcasted_iota(jnp.int32, (rows, LANES), 1)
    tile = jnp.zeros((rows, LANES), F32)
    for index, column in enumerate(columns):
        tile = jnp.where(lane == index, column, tile)
    return tile


def teacher_kernel(logits_ref, coeff_ref, out_ref):
    rows = logits_ref.shape[0]
    groups, _, part, _ = out_ref.shape
    blocks = coeff_ref.shape[0]

    def top(b, carry):
        return jnp.maximum(carry, logits_ref[:, pl.ds(pl.multiple_of(b * LANES, LANES), LANES)])

    widest = lax.fori_loop(
        1, blocks, top, logits_ref[:, 0:LANES], unroll=4
    ).astype(F32)
    row_max = jnp.max(widest, axis=1, keepdims=True)

    def one(b, total):
        x = logits_ref[:, pl.ds(pl.multiple_of(b * LANES, LANES), LANES)].astype(F32)
        e = jnp.exp(x - row_max)
        mapped = jnp.dot(e.astype(BF16), coeff_ref[b], preferred_element_type=F32).astype(BF16)
        out_ref[:, b] = mapped.reshape(groups, part, LANES)
        return total + e

    total = lax.fori_loop(0, blocks, one, jnp.zeros((rows, LANES), F32), unroll=4)
    row_total = jnp.sum(total, axis=1, keepdims=True)
    tile = lanes_of((row_max,) + pieces(row_total), rows).astype(BF16)
    out_ref[:, blocks] = tile.reshape(groups, part, LANES)


def collect_kernel(slot_ref, in_ref, out_ref, mass_ref, sums, scales):
    voc_count, held, part, _ = in_ref.shape
    blocks = held - 1
    slots = out_ref.shape[0]
    tops, totals = [], []
    for v in range(voc_count):
        tile = in_ref[v, blocks].astype(F32)
        tops.append(tile[:, 0:1])
        totals.append(tile[:, 1:2] + tile[:, 2:3] + tile[:, 3:4])
    top = functools.reduce(jnp.maximum, tops)
    total = functools.reduce(
        jnp.add, [part_total * jnp.exp(part_top - top) for part_total, part_top in zip(totals, tops)]
    )
    for v in range(voc_count):
        scales[v] = jnp.broadcast_to(jnp.exp(tops[v] - top) / total, (part, LANES))

    def clear(s, carry):
        sums[s] = jnp.zeros((part, LANES), F32)
        return carry

    lax.fori_loop(0, slots, clear, 0, unroll=8)
    for v in range(voc_count):
        scale = scales[v]

        def add(b, carry):
            slot = slot_ref[v * blocks + b]
            sums[slot] = sums[slot] + scale * in_ref[v, b].astype(F32)
            return carry

        lax.fori_loop(0, blocks, add, 0, unroll=4)

    def store(s, mass):
        target = sums[s].astype(BF16)
        out_ref[s] = target
        return mass + target.astype(F32)

    mass = lax.fori_loop(0, slots, store, jnp.zeros((part, LANES), F32), unroll=8)
    mass_ref[...] = jnp.broadcast_to(jnp.sum(mass, axis=1, keepdims=True), (part, LANES))


def logits_kernel(hidden_ref, weight_ref, mass_ref, logits_ref, stats_ref, tops, totals):
    step = pl.program_id(0)
    rows, cols = logits_ref.shape[1:]

    @pl.when(step == 0)
    def _():
        tops[...] = jnp.full(tops.shape, -jnp.inf, F32)
        totals[...] = jnp.zeros(totals.shape, F32)

    logits = jnp.dot(hidden_ref[...], weight_ref[0], preferred_element_type=F32)
    logits_ref[0] = logits
    tiles = [logits[:, k : k + LANES] for k in range(0, cols, LANES)]
    old = tops[...]
    new = functools.reduce(jnp.maximum, tiles, old)
    total = totals[...] * jnp.exp(old - new)
    for tile in tiles:
        total = total + jnp.exp(tile - new)
    tops[...] = new
    totals[...] = total

    @pl.when(step == pl.num_programs(0) - 1)
    def _():
        lane_top, lane_total = tops[...], totals[...]
        top = jnp.max(lane_top, axis=1, keepdims=True)
        total = jnp.sum(lane_total * jnp.exp(lane_top - top), axis=1, keepdims=True)
        part = mass_ref.shape[0]
        flat = jnp.transpose(lanes_of((top, total), rows))
        mass = jnp.transpose(mass_ref[...])
        mass = jnp.concatenate([mass[0:1], jnp.zeros((1, rows - part), F32)], axis=1)
        packed = jnp.concatenate([flat[0:2], mass, jnp.zeros((1, rows), F32)], axis=0)
        stats_ref[...] = jnp.broadcast_to(packed[None], stats_ref.shape)


def grad_kernel(
    first, place_ref, slot_ref, order_ref, stats_ref, logits_ref, target_ref, hidden_ref, hidden_t_ref,
    weight_ref, *rest
):
    if first:
        dweight_ref, partial, cross, norm, mass, gain = rest
    else:
        partial_in, cross_in, send_ref, keep_ref, dhidden_ref, base_ref = rest[:6]
        partial, cross, norm, mass, gain = rest[6:]
    step = pl.program_id(0)
    steps = pl.num_programs(0)
    group = order_ref[step]
    count, _, part, _ = target_ref.shape
    rows, cols = logits_ref.shape[1:]
    width = weight_ref.shape[1]

    @pl.when(step == 0)
    def _():
        tops = stats_ref[:, 0, :]
        top = jnp.max(tops, axis=0, keepdims=True)
        total = jnp.sum(stats_ref[:, 1, :] * jnp.exp(tops - top), axis=0, keepdims=True)
        norm[...] = jnp.transpose(jnp.broadcast_to(top + jnp.log(total), (LANES, rows)))
        own = stats_ref[:, 2, 0:LANES]
        wide_own = jnp.broadcast_to(own[:, None, :], (count, part, LANES))
        diagonal = lax.broadcasted_iota(jnp.int32, (count, part, LANES), 1) == lax.broadcasted_iota(
            jnp.int32, (count, part, LANES), 2
        )
        column = jnp.sum(jnp.where(diagonal, wide_own, 0.0), axis=2, keepdims=True).reshape(rows, 1)
        mass[...] = jnp.broadcast_to(column, (rows, LANES))
        gain[...] = jnp.broadcast_to(
            hidden_ref[:, width : width + LANES].astype(F32)[:, 0:1], (rows, LANES)
        )
        if first:
            cross[...] = jnp.zeros(cross.shape, F32)
        else:
            cross[...] = cross_in[...]

    norm_tile, mass_tile, gain_tile = norm[...], mass[...], gain[...]
    crossed = cross[...]
    grads = []
    for q in range(cols // LANES):
        logit = logits_ref[0, :, q * LANES : (q + 1) * LANES]
        slot = slot_ref[group * 2 * (cols // LANES) + (0 if first else cols // LANES) + q]
        held = target_ref[:, jnp.maximum(slot, 0)].reshape(rows, LANES).astype(F32)
        target = jnp.where(slot >= 0, held, 0.0)
        crossed = crossed + target * logit
        grads.append(
            (gain_tile * (mass_tile * jnp.exp(logit - norm_tile) - target)).astype(BF16)
        )
    cross[...] = crossed
    grad = jnp.concatenate(grads, axis=1)
    dweight = jnp.dot(hidden_t_ref[...], grad, preferred_element_type=F32).astype(BF16)
    if first:
        dweight_ref[0] = dweight
    else:

        @pl.when(step < steps // 2)
        def _():
            send_ref[0] = dweight

        @pl.when(step >= steps // 2)
        def _():
            keep_ref[0] = dweight

    product = lax.dot_general(
        grad, weight_ref[0], (((1,), (1,)), ((), ())), preferred_element_type=F32
    )

    @pl.when(step == 0)
    def _():
        if first:
            partial[...] = product
        else:
            partial[...] = partial_in[...] + product

    @pl.when(step > 0)
    def _():
        partial[...] = partial[...] + product

    if not first:

        @pl.when(step == steps - 1)
        def _():
            cross_sum = jnp.sum(cross[...], axis=1, keepdims=True)
            cross[...] = lanes_of(pieces(cross_sum), rows)
            for t in range(count):
                c = place_ref[t]
                dhidden_ref[c, :, 0:width] = partial[t * part : (t + 1) * part, :].astype(BF16)
                dhidden_ref[c, :, width : width + LANES] = cross[
                    t * part : (t + 1) * part, :
                ].astype(BF16)
            mass[...] = mass[...] * norm[...]
            start = pl.multiple_of(place_ref[count] * part, part)
            base_ref[...] = mass[pl.ds(start, part), :]


def half_grads(first, scalars, stats, logits, arrived, hidden_rows, hidden_t, weights, carried):
    voc_count, rows, cols = logits.shape
    ctx_count, capacity, part, _ = arrived.shape
    width = hidden_t.shape[0]
    half = cols // 2
    side = 0 if first else 1
    steps = voc_count // 2
    in_specs = [
        whole((ctx_count, 4, rows)),
        pl.BlockSpec((1, rows, half), lambda j, place, slot, order: (order[j], 0, side)),
        whole((ctx_count, capacity, part, LANES)),
        whole((rows, width + LANES)),
        whole((width, rows)),
        pl.BlockSpec((1, width, half), lambda j, place, slot, order: (order[j], 0, side)),
    ]
    state_shapes = (
        jax.ShapeDtypeStruct((rows, width), F32),
        jax.ShapeDtypeStruct((rows, LANES), F32),
    )
    columns = pltpu.VMEM((rows, LANES), F32)
    if first:
        out_shape = (jax.ShapeDtypeStruct((voc_count, width, half), BF16),) + state_shapes
        out_specs = (
            pl.BlockSpec((1, width, half), lambda j, *_: (j, 0, 0)),
            whole((rows, width)),
            whole((rows, LANES)),
        )
        scratch = [columns] * 3
    else:
        in_specs += [whole((rows, width)), whole((rows, LANES))]
        out_shape = (
            jax.ShapeDtypeStruct((steps, width, half), BF16),
            jax.ShapeDtypeStruct((steps, width, half), BF16),
            jax.ShapeDtypeStruct((ctx_count, part, width + LANES), BF16),
            jax.ShapeDtypeStruct((part, LANES), F32),
        )
        out_specs = (
            pl.BlockSpec((1, width, half), lambda j, *_: (jnp.minimum(j, steps - 1), 0, 0)),
            pl.BlockSpec((1, width, half), lambda j, *_: (jnp.maximum(j - steps, 0), 0, 0)),
            whole((ctx_count, part, width + LANES)),
            whole((part, LANES)),
        )
        scratch = [pltpu.VMEM((rows, width), F32)] + [columns] * 4
    return pl.pallas_call(
        functools.partial(grad_kernel, first),
        grid_spec=pltpu.PrefetchScalarGridSpec(
            num_scalar_prefetch=3,
            grid=(voc_count,),
            in_specs=in_specs,
            out_specs=out_specs,
            scratch_shapes=scratch,
        ),
        out_shape=out_shape,
        compiler_params=params(),
        cost_estimate=pl.CostEstimate(
            flops=2 * rows * width * cols * voc_count,
            bytes_accessed=15 * 1024 * 1024,
            transcendentals=rows * half * voc_count,
        ),
        name="grads_first" if first else "grads_second",
    )(*scalars, stats, logits, arrived, hidden_rows, hidden_t, weights, *carried)


def pair_kernel(a_ref, b_ref, out_ref):
    out_ref[...] = (a_ref[...].astype(F32) + b_ref[...].astype(F32)).astype(BF16)


def weight_kernel(first_ref, second_ref, out_ref):
    half = first_ref.shape[-1]
    out_ref[:, 0:half] = first_ref[...].astype(F32)
    total = second_ref[0].astype(F32)
    for k in range(1, second_ref.shape[0]):
        total = total + second_ref[k].astype(F32)
    out_ref[:, half : 2 * half] = total


def rows_kernel(turned_ref, in_ref, rows_ref, loss_ref):
    count, part, wide = in_ref.shape
    width = wide - LANES
    for v in range(count):
        got = in_ref[(v + turned_ref[0]) % count]
        rows_ref[v * part : (v + 1) * part, :] = got[:, 0:width]
        tail = got[:, width:wide].astype(F32)
        loss_ref[v * part : (v + 1) * part, :] = jnp.broadcast_to(
            tail[:, 0:1] + tail[:, 1:2] + tail[:, 2:3], (part, LANES)
        )


def stack_kernel(*refs):
    out_ref = refs[-1]
    part = refs[0].shape[0]
    for k, ref in enumerate(refs[:-1]):
        out_ref[k * part : (k + 1) * part, :] = ref[...]


def arrange_kernel(behind_ref, *refs):
    out_ref, held = refs[-2:]
    near = refs[0].shape[0]
    for k, ref in enumerate(refs[:-2]):
        held[k * near : (k + 1) * near] = ref[...]
    for t in range(out_ref.shape[0]):
        out_ref[t] = held[behind_ref[t]]


def fold(refs):
    wide = refs[0].shape[-1]
    total = refs[0][...].astype(F32)
    for ref in refs[1:]:
        total = total + ref[...].astype(F32)
    tail = total[:, wide - LANES :]
    return total[:, : wide - LANES], tail[:, 0:1] + tail[:, 1:2] + tail[:, 2:3]


def fold_kernel(*refs):
    out_ref = refs[-1]
    rows, wide = out_ref.shape
    total, crossed = fold(refs[:-1])
    out_ref[:, 0 : wide - LANES] = total.astype(BF16)
    out_ref[:, wide - LANES : wide] = lanes_of(pieces(crossed), rows).astype(BF16)


def finish_kernel(*refs):
    base_ref, out_ref = refs[-2:]
    rows, wide = out_ref.shape
    total, crossed = fold(refs[:-2])
    out_ref[:, 0 : wide - LANES] = total.astype(BF16)
    loss = base_ref[:, 0:1] - crossed
    out_ref[:, wide - LANES : wide] = lanes_of(pieces(loss), rows).astype(BF16)


def whole(shape):
    return pl.BlockSpec(shape, lambda *_: (0,) * len(shape))


def shifted(value, ring, along_x, step):
    count = lax.axis_size("ctx")
    lines = count // ring
    pairs = []
    for x in range(lines):
        for z in range(ring):
            to = (x + step) % lines * ring + z if along_x else x * ring + (z + step) % ring
            pairs.append((x * ring + z, to))
    return lax.ppermute(value, "ctx", pairs)


def spread(value, ring, along_x):
    count = lax.axis_size("ctx") // ring if along_x else ring
    return [value] + [shifted(value, ring, along_x, step) for step in range(1, count)]


def exchange(
    capacity, ring, head_weight, incoming, compact_slot, whole_slot, own_slot, place, behind, *lines
):
    ctx_count = lax.axis_size("ctx")
    voc_count, held, part, _ = incoming.shape
    width, cols = head_weight.shape
    dev_blocks = cols // LANES
    owned_blocks = voc_count * dev_blocks
    rows = ctx_count * part
    slots = ctx_count * capacity
    wide = width + LANES
    smem = pl.BlockSpec(memory_space=pltpu.SMEM)

    weights = lax.all_gather(head_weight, "voc", axis=0, tiled=False)
    slot = compact_slot if capacity == COMPACT else whole_slot
    target, mass = pl.pallas_call(
        collect_kernel,
        out_shape=(
            jax.ShapeDtypeStruct((slots, part, LANES), BF16),
            jax.ShapeDtypeStruct((part, LANES), F32),
        ),
        in_specs=[smem, pl.BlockSpec(memory_space=pltpu.VMEM)],
        scratch_shapes=[
            pltpu.VMEM((slots, part, LANES), F32),
            pltpu.VMEM((voc_count, part, LANES), F32),
        ],
        compiler_params=params(),
        cost_estimate=pl.CostEstimate(
            flops=4 * slots * part * LANES, bytes_accessed=6 * 1024 * 1024, transcendentals=0
        ),
        name="collect_targets",
    )(slot, incoming)
    target = target.reshape(ctx_count, capacity, part, LANES)
    arrived = lax.all_to_all(target, "ctx", 0, 0, tiled=True)
    hidden_rows = pl.pallas_call(
        arrange_kernel,
        out_shape=jax.ShapeDtypeStruct((ctx_count, part, wide), BF16),
        in_specs=[smem] + [pl.BlockSpec(memory_space=pltpu.VMEM)] * len(lines),
        scratch_shapes=[pltpu.VMEM((ctx_count, part, wide), BF16)],
        compiler_params=params(),
        name="arrange_rows",
    )(behind, *[line.reshape(ring, part, wide) for line in lines]).reshape(rows, wide)
    hidden_t = hidden_rows[:, :width].T

    logits, stats = pl.pallas_call(
        logits_kernel,
        grid=(voc_count,),
        in_specs=[
            pl.BlockSpec((rows, width), lambda j: (0, 0)),
            pl.BlockSpec((1, width, cols), lambda j: (j, 0, 0)),
            whole((part, LANES)),
        ],
        out_specs=(
            pl.BlockSpec((1, rows, cols), lambda j: (j, 0, 0)),
            whole((ctx_count, 4, rows)),
        ),
        out_shape=(
            jax.ShapeDtypeStruct((voc_count, rows, cols), F32),
            jax.ShapeDtypeStruct((ctx_count, 4, rows), F32),
        ),
        scratch_shapes=[pltpu.VMEM((rows, LANES), F32)] * 2,
        compiler_params=params(),
        cost_estimate=pl.CostEstimate(
            flops=2 * rows * width * cols * voc_count,
            bytes_accessed=18 * 1024 * 1024,
            transcendentals=rows * cols * voc_count,
        ),
        name="student_logits",
    )(hidden_rows, weights, mass)
    all_stats = lax.all_to_all(stats, "ctx", 0, 0, tiled=True)

    voc_index = lax.axis_index("voc")
    core = voc_index % 2
    lane_y = jnp.arange(voc_count // 2, dtype=jnp.int32)
    order = jnp.concatenate([2 * lane_y + 1 - core, 2 * lane_y + core]).astype(jnp.int32)
    straight = jnp.arange(voc_count, dtype=jnp.int32)
    dweight, partial, cross = half_grads(
        True, (place, own_slot, straight), all_stats, logits, arrived, hidden_rows, hidden_t, weights, ()
    )
    first_half = lax.psum_scatter(dweight, "voc", scatter_dimension=0, tiled=True)
    send, keep, dhidden, base = half_grads(
        False, (place, own_slot, order), all_stats, logits, arrived, hidden_rows, hidden_t, weights,
        (partial, cross),
    )
    got = lax.ppermute(send, "voc", [(v, v ^ 1) for v in range(voc_count)])
    quarter = pl.BlockSpec((1, width, cols // 2), lambda j: (j, 0, 0))
    summed = pl.pallas_call(
        pair_kernel,
        grid=(voc_count // 2,),
        in_specs=[quarter, quarter],
        out_specs=quarter,
        out_shape=jax.ShapeDtypeStruct((voc_count // 2, width, cols // 2), BF16),
        compiler_params=params(),
        name="sum_pair",
    )(keep, got)
    second_half = lax.all_to_all(
        summed, "voc", 0, 0, tiled=True,
        axis_index_groups=[list(range(k, voc_count, 2)) for k in range(2)],
    )
    pieces_x = dhidden.reshape(ctx_count // ring, ring * part, wide)
    parts = [pieces_x[0]]
    parts += [shifted(pieces_x[e], ring, True, e) for e in range(1, ctx_count // ring)]
    folded = pl.pallas_call(
        fold_kernel,
        out_shape=jax.ShapeDtypeStruct((ring * part, wide), BF16),
        compiler_params=params(),
        name="fold_rows",
    )(*parts)
    pieces_z = folded.reshape(ring, part, wide)
    parts = [pieces_z[0]] + [shifted(pieces_z[e], ring, False, e) for e in range(1, ring)]
    done = pl.pallas_call(
        finish_kernel,
        out_shape=jax.ShapeDtypeStruct((part, wide), BF16),
        compiler_params=params(),
        name="finish_rows",
    )(*parts, base)
    all_done = lax.all_gather(done, "voc", axis=0, tiled=False)
    turned = (lax.axis_index("ctx") % 2 * (voc_count // 2)).astype(jnp.int32)
    grad_hidden, loss_tile = pl.pallas_call(
        rows_kernel,
        in_specs=[smem, pl.BlockSpec(memory_space=pltpu.VMEM)],
        out_shape=(
            jax.ShapeDtypeStruct((voc_count * part, width), BF16),
            jax.ShapeDtypeStruct((voc_count * part, LANES), F32),
        ),
        compiler_params=params(),
        name="own_rows",
    )(turned[None], all_done)
    tall = width // 4
    grad_weight = pl.pallas_call(
        weight_kernel,
        grid=(4,),
        in_specs=[
            pl.BlockSpec((tall, cols // 2), lambda j: (j, 0)),
            pl.BlockSpec((voc_count // 2, tall, cols // 2), lambda j: (0, j, 0)),
        ],
        out_specs=pl.BlockSpec((tall, cols), lambda j: (j, 0)),
        out_shape=jax.ShapeDtypeStruct((width, cols), F32),
        compiler_params=params(),
        name="grad_weight",
    )(first_half.reshape(width, cols // 2), second_half)
    return grad_hidden, grad_weight, loss_tile


def local(hidden, token_weight, head_weight, teacher_logits, block_coeff, block_map):
    ctx_count = lax.axis_size("ctx")
    voc_count = lax.axis_size("voc")
    voc_index = lax.axis_index("voc")
    ctx_index = lax.axis_index("ctx")
    rows_dev, width = hidden.shape
    half_rows = rows_dev // 2
    part = rows_dev // voc_count
    half_groups = voc_count // 2
    local_blocks = block_coeff.shape[0]
    cols = head_weight.shape[1]
    dev_blocks = cols // LANES
    owned_blocks = voc_count * dev_blocks
    slots = ctx_count * owned_blocks
    rows = ctx_count * part
    wide = width + LANES

    parity = voc_index // half_groups
    fold_side = jnp.where(ctx_index % 2 == parity, 0, 1)
    start = fold_side * half_rows + voc_index % half_groups * part
    mine = lax.dynamic_slice_in_dim(hidden, start, part, 0)
    mine_weight = lax.dynamic_slice_in_dim(token_weight, start, part, 0)
    mine = jnp.concatenate([mine, jnp.broadcast_to(mine_weight[:, None], (part, LANES))], axis=1)
    ring = min(8, ctx_count)
    outgoing = pl.pallas_call(
        teacher_kernel,
        out_shape=jax.ShapeDtypeStruct((voc_count, local_blocks + 1, part, LANES), BF16),
        compiler_params=params(),
        cost_estimate=pl.CostEstimate(
            flops=2 * rows_dev * local_blocks * LANES * LANES,
            bytes_accessed=6 * 1024 * 1024,
            transcendentals=rows_dev * local_blocks * LANES,
        ),
        name="teacher_map",
    )(teacher_logits, block_coeff)
    outgoing, mine = lax.optimization_barrier((outgoing, mine))
    near = pl.pallas_call(
        stack_kernel,
        out_shape=jax.ShapeDtypeStruct((ring * part, wide), BF16),
        compiler_params=params(),
        name="stack_rows",
    )(*spread(mine, ring, False))
    incoming = lax.all_to_all(outgoing, "voc", 0, 0, tiled=True)

    wanted = jnp.any(
        block_map[:, None] == jnp.arange(slots, dtype=jnp.int32)[None, :], axis=0
    ).astype(jnp.int32).reshape(ctx_count, owned_blocks)
    number = jnp.cumsum(wanted, axis=1) - wanted
    fits = jnp.max(jnp.sum(wanted, axis=1)) <= COMPACT
    own_slot = jnp.where(wanted == 1, number, -1)
    own_slot = lax.dynamic_index_in_dim(own_slot, ctx_index, 0, keepdims=False)
    in_order = number.reshape(slots)[block_map]
    compact_slot = block_map // owned_blocks * COMPACT + in_order
    whole_slot = block_map // owned_blocks * owned_blocks + in_order

    source = jnp.arange(ctx_count, dtype=jnp.int32)
    half_block = 2 * source + parity
    place = jnp.where(half_block < ctx_count, half_block, 2 * ctx_count - 1 - half_block)
    own_half = jnp.where(fold_side == 0, ctx_index, 2 * ctx_count - 1 - ctx_index)
    behind = (ctx_index // ring - place // ring) % (ctx_count // ring) * ring + (ctx_index - place) % ring
    ahead = (place // ring - ctx_index // ring) % (ctx_count // ring) * ring + (place - ctx_index) % ring
    place = jnp.concatenate([ahead, (own_half // 2)[None]]).astype(jnp.int32)
    lines = spread(near, ring, True)
    operands = lax.optimization_barrier(
        (incoming, compact_slot, whole_slot, own_slot, place, behind, *lines)
    )
    grad_hidden, grad_weight, loss_tile = lax.cond(
        fits,
        functools.partial(exchange, COMPACT, ring),
        functools.partial(exchange, owned_blocks, ring),
        head_weight,
        *operands,
    )
    row_loss = loss_tile[:, 0]
    return (grad_hidden, grad_weight, row_loss)


def solution(mesh):
    return jax.shard_map(
        local,
        mesh=mesh,
        in_specs=(
            P("ctx", None),
            P("ctx"),
            P(None, ("ctx", "voc")),
            P("ctx", "voc"),
            P("voc", None, None),
            P(),
        ),
        out_specs=(P("ctx", None), P(None, ("ctx", "voc")), P("ctx")),
        check_vma=False,
    )
```

```python
import functools

import jax
import jax.numpy as jnp
from jax import lax
from jax.experimental import pallas as pl
from jax.experimental.pallas import tpu as pltpu
from jax.sharding import PartitionSpec as P

F32 = jnp.float32
BF16 = jnp.bfloat16
LANES = 128
COMPACT = 20
MIB = 1024 * 1024


def params(mib=8):
    return pltpu.CompilerParams(vmem_limit_bytes=mib * MIB)


def pieces(value):
    high = value.astype(BF16).astype(F32)
    rest = value - high
    middle = rest.astype(BF16).astype(F32)
    return high, middle, rest - middle


def lanes_of(columns, rows):
    lane = lax.broadcasted_iota(jnp.int32, (rows, LANES), 1)
    tile = jnp.zeros((rows, LANES), F32)
    for index, column in enumerate(columns):
        tile = jnp.where(lane == index, column, tile)
    return tile


def teacher_kernel(logits_ref, coeff_ref, out_ref):
    rows = logits_ref.shape[0]
    groups, _, part, _ = out_ref.shape
    blocks = coeff_ref.shape[0]

    def top(b, carry):
        return jnp.maximum(carry, logits_ref[:, pl.ds(pl.multiple_of(b * LANES, LANES), LANES)])

    widest = lax.fori_loop(
        1, blocks, top, logits_ref[:, 0:LANES], unroll=4
    ).astype(F32)
    row_max = jnp.max(widest, axis=1, keepdims=True)

    def one(b, total):
        x = logits_ref[:, pl.ds(pl.multiple_of(b * LANES, LANES), LANES)].astype(F32)
        e = jnp.exp(x - row_max)
        mapped = jnp.dot(e.astype(BF16), coeff_ref[b], preferred_element_type=F32).astype(BF16)
        out_ref[:, b] = mapped.reshape(groups, part, LANES)
        return total + e

    total = lax.fori_loop(0, blocks, one, jnp.zeros((rows, LANES), F32), unroll=4)
    row_total = jnp.sum(total, axis=1, keepdims=True)
    tile = lanes_of((row_max,) + pieces(row_total), rows).astype(BF16)
    out_ref[:, blocks] = tile.reshape(groups, part, LANES)


def collect_kernel(slot_ref, in_ref, out_ref, mass_ref, sums, scales):
    voc_count, held, part, _ = in_ref.shape
    blocks = held - 1
    slots = out_ref.shape[0]
    tops, totals = [], []
    for v in range(voc_count):
        tile = in_ref[v, blocks].astype(F32)
        tops.append(tile[:, 0:1])
        totals.append(tile[:, 1:2] + tile[:, 2:3] + tile[:, 3:4])
    top = functools.reduce(jnp.maximum, tops)
    total = functools.reduce(
        jnp.add, [part_total * jnp.exp(part_top - top) for part_total, part_top in zip(totals, tops)]
    )
    for v in range(voc_count):
        scales[v] = jnp.broadcast_to(jnp.exp(tops[v] - top) / total, (part, LANES))

    def clear(s, carry):
        sums[s] = jnp.zeros((part, LANES), F32)
        return carry

    lax.fori_loop(0, slots, clear, 0, unroll=8)
    for v in range(voc_count):
        scale = scales[v]

        def add(b, carry):
            slot = slot_ref[v * blocks + b]
            sums[slot] = sums[slot] + scale * in_ref[v, b].astype(F32)
            return carry

        lax.fori_loop(0, blocks, add, 0, unroll=4)

    def store(s, mass):
        target = sums[s].astype(BF16)
        out_ref[s] = target
        return mass + target.astype(F32)

    mass = lax.fori_loop(0, slots, store, jnp.zeros((part, LANES), F32), unroll=8)
    mass_ref[...] = jnp.broadcast_to(jnp.sum(mass, axis=1, keepdims=True), (part, LANES))


def logits_kernel(hidden_ref, weight_ref, mass_ref, logits_ref, stats_ref, tops, totals):
    step = pl.program_id(0)
    rows, cols = logits_ref.shape[1:]

    @pl.when(step == 0)
    def _():
        tops[...] = jnp.full(tops.shape, -jnp.inf, F32)
        totals[...] = jnp.zeros(totals.shape, F32)

    logits = jnp.dot(hidden_ref[...], weight_ref[0], preferred_element_type=F32)
    logits_ref[0] = logits
    tiles = [logits[:, k : k + LANES] for k in range(0, cols, LANES)]
    old = tops[...]
    new = functools.reduce(jnp.maximum, tiles, old)
    total = totals[...] * jnp.exp(old - new)
    for tile in tiles:
        total = total + jnp.exp(tile - new)
    tops[...] = new
    totals[...] = total

    @pl.when(step == pl.num_programs(0) - 1)
    def _():
        lane_top, lane_total = tops[...], totals[...]
        top = jnp.max(lane_top, axis=1, keepdims=True)
        total = jnp.sum(lane_total * jnp.exp(lane_top - top), axis=1, keepdims=True)
        part = mass_ref.shape[0]
        flat = jnp.transpose(lanes_of((top, total), rows))
        mass = jnp.transpose(mass_ref[...])
        mass = jnp.concatenate([mass[0:1], jnp.zeros((1, rows - part), F32)], axis=1)
        packed = jnp.concatenate([flat[0:2], mass, jnp.zeros((1, rows), F32)], axis=0)
        stats_ref[...] = jnp.broadcast_to(packed[None], stats_ref.shape)


def grad_kernel(
    place_ref, slot_ref, stats_ref, logits_ref, target_ref, hidden_ref, hidden_t_ref, weight_ref,
    dweight_ref, dhidden_ref, base_ref, norm, mass, gain, cross, partial,
):
    step = pl.program_id(0)
    count, _, part, _ = target_ref.shape
    rows, cols = logits_ref.shape[1:]
    width = weight_ref.shape[1]

    @pl.when(step == 0)
    def _():
        tops = stats_ref[:, 0, :]
        top = jnp.max(tops, axis=0, keepdims=True)
        total = jnp.sum(stats_ref[:, 1, :] * jnp.exp(tops - top), axis=0, keepdims=True)
        norm_row = jnp.broadcast_to(top + jnp.log(total), (LANES, rows))
        norm[...] = jnp.transpose(norm_row)
        own = stats_ref[:, 2, 0:LANES]
        spread = jnp.broadcast_to(own[:, None, :], (count, part, LANES))
        diagonal = lax.broadcasted_iota(jnp.int32, (count, part, LANES), 1) == lax.broadcasted_iota(
            jnp.int32, (count, part, LANES), 2
        )
        column = jnp.sum(jnp.where(diagonal, spread, 0.0), axis=2, keepdims=True).reshape(rows, 1)
        mass[...] = jnp.broadcast_to(column, (rows, LANES))
        gain[...] = jnp.broadcast_to(
            hidden_ref[:, width : width + LANES].astype(F32)[:, 0:1], (rows, LANES)
        )
        cross[...] = jnp.zeros(cross.shape, F32)

    norm_tile, mass_tile, gain_tile = norm[...], mass[...], gain[...]
    crossed = cross[...]
    grads = []
    for q in range(cols // LANES):
        logit = logits_ref[0, :, q * LANES : (q + 1) * LANES]
        slot = slot_ref[step * (cols // LANES) + q]
        held = target_ref[:, jnp.maximum(slot, 0)].reshape(rows, LANES).astype(F32)
        target = jnp.where(slot >= 0, held, 0.0)
        crossed = crossed + target * logit
        grads.append(
            (gain_tile * (mass_tile * jnp.exp(logit - norm_tile) - target)).astype(BF16)
        )
    cross[...] = crossed
    grad = jnp.concatenate(grads, axis=1)
    dweight_ref[0] = jnp.dot(hidden_t_ref[...], grad, preferred_element_type=F32).astype(BF16)
    product = lax.dot_general(
        grad, weight_ref[0], (((1,), (1,)), ((), ())), preferred_element_type=F32
    )

    @pl.when(step == 0)
    def _():
        partial[...] = product

    @pl.when(step > 0)
    def _():
        partial[...] = partial[...] + product

    @pl.when(step == pl.num_programs(0) - 1)
    def _():
        cross_sum = jnp.sum(cross[...], axis=1, keepdims=True)
        cross[...] = lanes_of(pieces(cross_sum), rows)
        for t in range(count):
            c = place_ref[t]
            dhidden_ref[c, :, 0:width] = partial[t * part : (t + 1) * part, :].astype(BF16)
            dhidden_ref[c, :, width : width + LANES] = cross[t * part : (t + 1) * part, :].astype(BF16)
        mass[...] = mass[...] * norm[...]
        start = pl.multiple_of(place_ref[count] * part, part)
        base_ref[...] = mass[pl.ds(start, part), :]


def rows_kernel(turned_ref, in_ref, rows_ref, loss_ref):
    count, part, wide = in_ref.shape
    width = wide - LANES
    for v in range(count):
        got = in_ref[(v + turned_ref[0]) % count]
        rows_ref[v * part : (v + 1) * part, :] = got[:, 0:width]
        tail = got[:, width:wide].astype(F32)
        loss_ref[v * part : (v + 1) * part, :] = jnp.broadcast_to(
            tail[:, 0:1] + tail[:, 1:2] + tail[:, 2:3], (part, LANES)
        )


def stack_kernel(*refs):
    out_ref = refs[-1]
    part = refs[0].shape[0]
    for k, ref in enumerate(refs[:-1]):
        out_ref[k * part : (k + 1) * part, :] = ref[...]


def arrange_kernel(behind_ref, *refs):
    out_ref, held = refs[-2:]
    near = refs[0].shape[0]
    for k, ref in enumerate(refs[:-2]):
        held[k * near : (k + 1) * near] = ref[...]
    for t in range(out_ref.shape[0]):
        out_ref[t] = held[behind_ref[t]]


def fold(refs):
    wide = refs[0].shape[-1]
    total = refs[0][...].astype(F32)
    for ref in refs[1:]:
        total = total + ref[...].astype(F32)
    tail = total[:, wide - LANES :]
    return total[:, : wide - LANES], tail[:, 0:1] + tail[:, 1:2] + tail[:, 2:3]


def fold_kernel(*refs):
    out_ref = refs[-1]
    rows, wide = out_ref.shape
    total, crossed = fold(refs[:-1])
    out_ref[:, 0 : wide - LANES] = total.astype(BF16)
    out_ref[:, wide - LANES : wide] = lanes_of(pieces(crossed), rows).astype(BF16)


def finish_kernel(*refs):
    base_ref, out_ref = refs[-2:]
    rows, wide = out_ref.shape
    total, crossed = fold(refs[:-2])
    out_ref[:, 0 : wide - LANES] = total.astype(BF16)
    loss = base_ref[:, 0:1] - crossed
    out_ref[:, wide - LANES : wide] = lanes_of(pieces(loss), rows).astype(BF16)


def whole(shape):
    return pl.BlockSpec(shape, lambda *_: (0,) * len(shape))


def shifted(value, ring, along_x, step):
    count = lax.axis_size("ctx")
    lines = count // ring
    pairs = []
    for x in range(lines):
        for z in range(ring):
            to = (x + step) % lines * ring + z if along_x else x * ring + (z + step) % ring
            pairs.append((x * ring + z, to))
    return lax.ppermute(value, "ctx", pairs)


def spread(value, ring, along_x):
    count = lax.axis_size("ctx") // ring if along_x else ring
    return [value] + [shifted(value, ring, along_x, step) for step in range(1, count)]


def exchange(
    capacity, ring, head_weight, incoming, compact_slot, whole_slot, own_slot, place, behind, *lines
):
    ctx_count = lax.axis_size("ctx")
    voc_count, held, part, _ = incoming.shape
    width, cols = head_weight.shape
    dev_blocks = cols // LANES
    owned_blocks = voc_count * dev_blocks
    rows = ctx_count * part
    slots = ctx_count * capacity
    wide = width + LANES
    smem = pl.BlockSpec(memory_space=pltpu.SMEM)

    weights = lax.all_gather(head_weight, "voc", axis=0, tiled=False)
    slot = compact_slot if capacity == COMPACT else whole_slot
    target, mass = pl.pallas_call(
        collect_kernel,
        out_shape=(
            jax.ShapeDtypeStruct((slots, part, LANES), BF16),
            jax.ShapeDtypeStruct((part, LANES), F32),
        ),
        in_specs=[smem, pl.BlockSpec(memory_space=pltpu.VMEM)],
        scratch_shapes=[
            pltpu.VMEM((slots, part, LANES), F32),
            pltpu.VMEM((voc_count, part, LANES), F32),
        ],
        compiler_params=params(20),
        cost_estimate=pl.CostEstimate(
            flops=4 * slots * part * LANES, bytes_accessed=6 * 1024 * 1024, transcendentals=0
        ),
        name="collect_targets",
    )(slot, incoming)
    target = target.reshape(ctx_count, capacity, part, LANES)
    arrived = lax.all_to_all(target, "ctx", 0, 0, tiled=True)
    hidden_rows = pl.pallas_call(
        arrange_kernel,
        out_shape=jax.ShapeDtypeStruct((ctx_count, part, wide), BF16),
        in_specs=[smem] + [pl.BlockSpec(memory_space=pltpu.VMEM)] * len(lines),
        scratch_shapes=[pltpu.VMEM((ctx_count, part, wide), BF16)],
        compiler_params=params(),
        name="arrange_rows",
    )(behind, *[line.reshape(ring, part, wide) for line in lines]).reshape(rows, wide)
    hidden_t = hidden_rows[:, :width].T

    logits, stats = pl.pallas_call(
        logits_kernel,
        grid=(voc_count,),
        in_specs=[
            pl.BlockSpec((rows, width), lambda j: (0, 0)),
            pl.BlockSpec((1, width, cols), lambda j: (j, 0, 0)),
            whole((part, LANES)),
        ],
        out_specs=(
            pl.BlockSpec((1, rows, cols), lambda j: (j, 0, 0)),
            whole((ctx_count, 4, rows)),
        ),
        out_shape=(
            jax.ShapeDtypeStruct((voc_count, rows, cols), F32),
            jax.ShapeDtypeStruct((ctx_count, 4, rows), F32),
        ),
        scratch_shapes=[pltpu.VMEM((rows, LANES), F32)] * 2,
        compiler_params=params(16),
        cost_estimate=pl.CostEstimate(
            flops=2 * rows * width * cols * voc_count,
            bytes_accessed=18 * 1024 * 1024,
            transcendentals=rows * cols * voc_count,
        ),
        name="student_logits",
    )(hidden_rows, weights, mass)
    all_stats = lax.all_to_all(stats, "ctx", 0, 0, tiled=True)

    dweight, dhidden, base = pl.pallas_call(
        grad_kernel,
        grid=(voc_count,),
        in_specs=[
            smem,
            smem,
            whole((ctx_count, 4, rows)),
            pl.BlockSpec((1, rows, cols), lambda j: (j, 0, 0)),
            whole((ctx_count, capacity, part, LANES)),
            whole((rows, width + LANES)),
            whole((width, rows)),
            pl.BlockSpec((1, width, cols), lambda j: (j, 0, 0)),
        ],
        out_specs=(
            pl.BlockSpec((1, width, cols), lambda j: (j, 0, 0)),
            whole((ctx_count, part, width + LANES)),
            whole((part, LANES)),
        ),
        out_shape=(
            jax.ShapeDtypeStruct((voc_count, width, cols), BF16),
            jax.ShapeDtypeStruct((ctx_count, part, width + LANES), BF16),
            jax.ShapeDtypeStruct((part, LANES), F32),
        ),
        scratch_shapes=[pltpu.VMEM((rows, LANES), F32)] * 4 + [pltpu.VMEM((rows, width), F32)],
        compiler_params=params(28),
        cost_estimate=pl.CostEstimate(
            flops=4 * rows * width * cols * voc_count,
            bytes_accessed=30 * 1024 * 1024,
            transcendentals=rows * cols * voc_count,
        ),
        name="grads",
    )(place, own_slot, all_stats, logits, arrived, hidden_rows, hidden_t, weights)
    return dweight, dhidden, base


def local(hidden, token_weight, head_weight, teacher_logits, block_coeff, block_map):
    ctx_count = lax.axis_size("ctx")
    voc_count = lax.axis_size("voc")
    voc_index = lax.axis_index("voc")
    ctx_index = lax.axis_index("ctx")
    rows_dev, width = hidden.shape
    half_rows = rows_dev // 2
    part = rows_dev // voc_count
    half_groups = voc_count // 2
    local_blocks = block_coeff.shape[0]
    cols = head_weight.shape[1]
    dev_blocks = cols // LANES
    owned_blocks = voc_count * dev_blocks
    slots = ctx_count * owned_blocks
    rows = ctx_count * part
    wide = width + LANES

    parity = voc_index // half_groups
    fold_side = jnp.where(ctx_index % 2 == parity, 0, 1)
    start = fold_side * half_rows + voc_index % half_groups * part
    mine = lax.dynamic_slice_in_dim(hidden, start, part, 0)
    mine_weight = lax.dynamic_slice_in_dim(token_weight, start, part, 0)
    mine = jnp.concatenate([mine, jnp.broadcast_to(mine_weight[:, None], (part, LANES))], axis=1)
    ring = min(8, ctx_count)
    outgoing = pl.pallas_call(
        teacher_kernel,
        out_shape=jax.ShapeDtypeStruct((voc_count, local_blocks + 1, part, LANES), BF16),
        compiler_params=params(12),
        cost_estimate=pl.CostEstimate(
            flops=2 * rows_dev * local_blocks * LANES * LANES,
            bytes_accessed=6 * 1024 * 1024,
            transcendentals=rows_dev * local_blocks * LANES,
        ),
        name="teacher_map",
    )(teacher_logits, block_coeff)
    outgoing, mine = lax.optimization_barrier((outgoing, mine))
    near = pl.pallas_call(
        stack_kernel,
        out_shape=jax.ShapeDtypeStruct((ring * part, wide), BF16),
        compiler_params=params(),
        name="stack_rows",
    )(*spread(mine, ring, False))
    incoming = lax.all_to_all(outgoing, "voc", 0, 0, tiled=True)

    wanted = jnp.any(
        block_map[:, None] == jnp.arange(slots, dtype=jnp.int32)[None, :], axis=0
    ).astype(jnp.int32).reshape(ctx_count, owned_blocks)
    number = jnp.cumsum(wanted, axis=1) - wanted
    fits = jnp.max(jnp.sum(wanted, axis=1)) <= COMPACT
    own_slot = jnp.where(wanted == 1, number, -1)
    own_slot = lax.dynamic_index_in_dim(own_slot, ctx_index, 0, keepdims=False)
    in_order = number.reshape(slots)[block_map]
    compact_slot = block_map // owned_blocks * COMPACT + in_order
    whole_slot = block_map // owned_blocks * owned_blocks + in_order

    source = jnp.arange(ctx_count, dtype=jnp.int32)
    half_block = 2 * source + parity
    place = jnp.where(half_block < ctx_count, half_block, 2 * ctx_count - 1 - half_block)
    own_half = jnp.where(fold_side == 0, ctx_index, 2 * ctx_count - 1 - ctx_index)
    behind = (ctx_index // ring - place // ring) % (ctx_count // ring) * ring + (ctx_index - place) % ring
    ahead = (place // ring - ctx_index // ring) % (ctx_count // ring) * ring + (place - ctx_index) % ring
    place = jnp.concatenate([ahead, (own_half // 2)[None]]).astype(jnp.int32)
    lines = spread(near, ring, True)
    operands = lax.optimization_barrier(
        (incoming, compact_slot, whole_slot, own_slot, place, behind, *lines)
    )
    dweight, dhidden, base = lax.cond(
        fits,
        functools.partial(exchange, COMPACT, ring),
        functools.partial(exchange, owned_blocks, ring),
        head_weight,
        *operands,
    )
    grad_weight = lax.psum_scatter(dweight, "voc", scatter_dimension=0, tiled=True)
    grad_weight = grad_weight.reshape(width, cols).astype(F32)
    pieces_x = dhidden.reshape(ctx_count // ring, ring * part, wide)
    parts = [pieces_x[0]]
    parts += [shifted(pieces_x[e], ring, True, e) for e in range(1, ctx_count // ring)]
    folded = pl.pallas_call(
        fold_kernel,
        out_shape=jax.ShapeDtypeStruct((ring * part, wide), BF16),
        compiler_params=params(),
        name="fold_rows",
    )(*parts)
    pieces_z = folded.reshape(ring, part, wide)
    parts = [pieces_z[0]] + [shifted(pieces_z[e], ring, False, e) for e in range(1, ring)]
    done = pl.pallas_call(
        finish_kernel,
        out_shape=jax.ShapeDtypeStruct((part, wide), BF16),
        compiler_params=params(),
        name="finish_rows",
    )(*parts, base)
    all_done = lax.all_gather(done, "voc", axis=0, tiled=False)
    turned = (ctx_index % 2 * half_groups).astype(jnp.int32)
    grad_hidden, loss_tile = pl.pallas_call(
        rows_kernel,
        in_specs=[
            pl.BlockSpec(memory_space=pltpu.SMEM),
            pl.BlockSpec(memory_space=pltpu.VMEM),
        ],
        out_shape=(
            jax.ShapeDtypeStruct((rows_dev, width), BF16),
            jax.ShapeDtypeStruct((rows_dev, LANES), F32),
        ),
        compiler_params=params(),
        name="own_rows",
    )(turned[None], all_done)
    row_loss = loss_tile[:, 0]
    return (grad_hidden, grad_weight, row_loss)


def solution(mesh):
    return jax.shard_map(
        local,
        mesh=mesh,
        in_specs=(
            P("ctx", None),
            P("ctx"),
            P(None, ("ctx", "voc")),
            P("ctx", "voc"),
            P("voc", None, None),
            P(),
        ),
        out_specs=(P("ctx", None), P(None, ("ctx", "voc")), P("ctx")),
        check_vma=False,
    )
```

```python
import functools

import jax
import jax.numpy as jnp
from jax import lax
from jax.experimental import pallas as pl
from jax.experimental.pallas import tpu as pltpu
from jax.sharding import PartitionSpec as P

F32 = jnp.float32
BF16 = jnp.bfloat16
LANES = 128
COMPACT = 20
MIB = 1024 * 1024


def params(mib=8):
    return pltpu.CompilerParams(vmem_limit_bytes=mib * MIB)


def pieces(value):
    high = value.astype(BF16).astype(F32)
    rest = value - high
    middle = rest.astype(BF16).astype(F32)
    return high, middle, rest - middle


def lanes_of(columns, rows):
    lane = lax.broadcasted_iota(jnp.int32, (rows, LANES), 1)
    tile = jnp.zeros((rows, LANES), F32)
    for index, column in enumerate(columns):
        tile = jnp.where(lane == index, column, tile)
    return tile


def teacher_kernel(logits_ref, coeff_ref, out_ref):
    rows = logits_ref.shape[0]
    groups, _, part, _ = out_ref.shape
    blocks = coeff_ref.shape[0]

    def top(b, carry):
        return jnp.maximum(carry, logits_ref[:, pl.ds(pl.multiple_of(b * LANES, LANES), LANES)])

    widest = lax.fori_loop(
        1, blocks, top, logits_ref[:, 0:LANES], unroll=4
    ).astype(F32)
    row_max = jnp.max(widest, axis=1, keepdims=True)

    def one(b, total):
        x = logits_ref[:, pl.ds(pl.multiple_of(b * LANES, LANES), LANES)].astype(F32)
        e = jnp.exp(x - row_max)
        mapped = jnp.dot(e.astype(BF16), coeff_ref[b], preferred_element_type=F32).astype(BF16)
        out_ref[:, b] = mapped.reshape(groups, part, LANES)
        return total + e

    total = lax.fori_loop(0, blocks, one, jnp.zeros((rows, LANES), F32), unroll=4)
    row_total = jnp.sum(total, axis=1, keepdims=True)
    tile = lanes_of((row_max,) + pieces(row_total), rows).astype(BF16)
    out_ref[:, blocks] = tile.reshape(groups, part, LANES)


def collect_kernel(slot_ref, in_ref, out_ref, mass_ref, sums, scales):
    voc_count, held, part, _ = in_ref.shape
    blocks = held - 1
    slots = out_ref.shape[0]
    tops, totals = [], []
    for v in range(voc_count):
        tile = in_ref[v, blocks].astype(F32)
        tops.append(tile[:, 0:1])
        totals.append(tile[:, 1:2] + tile[:, 2:3] + tile[:, 3:4])
    top = functools.reduce(jnp.maximum, tops)
    total = functools.reduce(
        jnp.add, [part_total * jnp.exp(part_top - top) for part_total, part_top in zip(totals, tops)]
    )
    for v in range(voc_count):
        scales[v] = jnp.broadcast_to(jnp.exp(tops[v] - top) / total, (part, LANES))

    def clear(s, carry):
        sums[s] = jnp.zeros((part, LANES), F32)
        return carry

    lax.fori_loop(0, slots, clear, 0, unroll=8)
    for v in range(voc_count):
        scale = scales[v]

        def add(b, carry):
            slot = slot_ref[v * blocks + b]
            sums[slot] = sums[slot] + scale * in_ref[v, b].astype(F32)
            return carry

        lax.fori_loop(0, blocks, add, 0, unroll=4)

    def store(s, mass):
        target = sums[s].astype(BF16)
        out_ref[s] = target
        return mass + target.astype(F32)

    mass = lax.fori_loop(0, slots, store, jnp.zeros((part, LANES), F32), unroll=8)
    mass_ref[...] = jnp.broadcast_to(jnp.sum(mass, axis=1, keepdims=True), (part, LANES))


def logits_kernel(hidden_ref, weight_ref, mass_ref, logits_ref, stats_ref, tops, totals):
    step = pl.program_id(0)
    rows, cols = logits_ref.shape[1:]

    @pl.when(step == 0)
    def _():
        tops[...] = jnp.full(tops.shape, -jnp.inf, F32)
        totals[...] = jnp.zeros(totals.shape, F32)

    logits = jnp.dot(hidden_ref[...], weight_ref[0], preferred_element_type=F32)
    logits_ref[0] = logits
    tiles = [logits[:, k : k + LANES] for k in range(0, cols, LANES)]
    old = tops[...]
    new = functools.reduce(jnp.maximum, tiles, old)
    total = totals[...] * jnp.exp(old - new)
    for tile in tiles:
        total = total + jnp.exp(tile - new)
    tops[...] = new
    totals[...] = total

    @pl.when(step == pl.num_programs(0) - 1)
    def _():
        lane_top, lane_total = tops[...], totals[...]
        top = jnp.max(lane_top, axis=1, keepdims=True)
        total = jnp.sum(lane_total * jnp.exp(lane_top - top), axis=1, keepdims=True)
        part = mass_ref.shape[0]
        flat = jnp.transpose(lanes_of((top, total), rows))
        mass = jnp.transpose(mass_ref[...])
        mass = jnp.concatenate([mass[0:1], jnp.zeros((1, rows - part), F32)], axis=1)
        packed = jnp.concatenate([flat[0:2], mass, jnp.zeros((1, rows), F32)], axis=0)
        stats_ref[...] = jnp.broadcast_to(packed[None], stats_ref.shape)


def grad_kernel(
    place_ref, slot_ref, stats_ref, logits_ref, target_ref, hidden_ref, hidden_t_ref, weight_ref,
    dweight_ref, dhidden_ref, base_ref, norm, mass, gain, cross, partial,
):
    step = pl.program_id(0)
    count, _, part, _ = target_ref.shape
    rows, cols = logits_ref.shape[1:]
    width = weight_ref.shape[1]

    @pl.when(step == 0)
    def _():
        tops = stats_ref[:, 0, :]
        top = jnp.max(tops, axis=0, keepdims=True)
        total = jnp.sum(stats_ref[:, 1, :] * jnp.exp(tops - top), axis=0, keepdims=True)
        norm_row = jnp.broadcast_to(top + jnp.log(total), (LANES, rows))
        norm[...] = jnp.transpose(norm_row)
        own = stats_ref[:, 2, 0:LANES]
        spread = jnp.broadcast_to(own[:, None, :], (count, part, LANES))
        diagonal = lax.broadcasted_iota(jnp.int32, (count, part, LANES), 1) == lax.broadcasted_iota(
            jnp.int32, (count, part, LANES), 2
        )
        column = jnp.sum(jnp.where(diagonal, spread, 0.0), axis=2, keepdims=True).reshape(rows, 1)
        mass[...] = jnp.broadcast_to(column, (rows, LANES))
        gain[...] = jnp.broadcast_to(
            hidden_ref[:, width : width + LANES].astype(F32)[:, 0:1], (rows, LANES)
        )
        cross[...] = jnp.zeros(cross.shape, F32)

    norm_tile, mass_tile, gain_tile = norm[...], mass[...], gain[...]
    crossed = cross[...]
    grads = []
    for q in range(cols // LANES):
        logit = logits_ref[0, :, q * LANES : (q + 1) * LANES]
        slot = slot_ref[step * (cols // LANES) + q]
        held = target_ref[:, jnp.maximum(slot, 0)].reshape(rows, LANES).astype(F32)
        target = jnp.where(slot >= 0, held, 0.0)
        crossed = crossed + target * logit
        grads.append(
            (gain_tile * (mass_tile * jnp.exp(logit - norm_tile) - target)).astype(BF16)
        )
    cross[...] = crossed
    grad = jnp.concatenate(grads, axis=1)
    dweight_ref[0] = jnp.dot(hidden_t_ref[...], grad, preferred_element_type=F32).astype(BF16)
    product = lax.dot_general(
        grad, weight_ref[0], (((1,), (1,)), ((), ())), preferred_element_type=F32
    )

    @pl.when(step == 0)
    def _():
        partial[...] = product

    @pl.when(step > 0)
    def _():
        partial[...] = partial[...] + product

    @pl.when(step == pl.num_programs(0) - 1)
    def _():
        cross_sum = jnp.sum(cross[...], axis=1, keepdims=True)
        cross[...] = lanes_of(pieces(cross_sum), rows)
        for t in range(count):
            c = place_ref[t]
            dhidden_ref[c, :, 0:width] = partial[t * part : (t + 1) * part, :].astype(BF16)
            dhidden_ref[c, :, width : width + LANES] = cross[t * part : (t + 1) * part, :].astype(BF16)
        mass[...] = mass[...] * norm[...]
        start = pl.multiple_of(place_ref[count] * part, part)
        base_ref[...] = mass[pl.ds(start, part), :]


def rows_kernel(turned_ref, in_ref, rows_ref, loss_ref):
    count, part, wide = in_ref.shape
    width = wide - LANES
    for v in range(count):
        got = in_ref[(v + turned_ref[0]) % count]
        rows_ref[v * part : (v + 1) * part, :] = got[:, 0:width]
        tail = got[:, width:wide].astype(F32)
        loss_ref[v * part : (v + 1) * part, :] = jnp.broadcast_to(
            tail[:, 0:1] + tail[:, 1:2] + tail[:, 2:3], (part, LANES)
        )


def stack_kernel(*refs):
    out_ref = refs[-1]
    part = refs[0].shape[0]
    for k, ref in enumerate(refs[:-1]):
        out_ref[k * part : (k + 1) * part, :] = ref[...]


def arrange_kernel(behind_ref, *refs):
    out_ref, held = refs[-2:]
    near = refs[0].shape[0]
    for k, ref in enumerate(refs[:-2]):
        held[k * near : (k + 1) * near] = ref[...]
    for t in range(out_ref.shape[0]):
        out_ref[t] = held[behind_ref[t]]


def fold(refs):
    wide = refs[0].shape[-1]
    total = refs[0][...].astype(F32)
    for ref in refs[1:]:
        total = total + ref[...].astype(F32)
    tail = total[:, wide - LANES :]
    return total[:, : wide - LANES], tail[:, 0:1] + tail[:, 1:2] + tail[:, 2:3]


def fold_kernel(*refs):
    out_ref = refs[-1]
    rows, wide = out_ref.shape
    total, crossed = fold(refs[:-1])
    out_ref[:, 0 : wide - LANES] = total.astype(BF16)
    out_ref[:, wide - LANES : wide] = lanes_of(pieces(crossed), rows).astype(BF16)


def finish_kernel(*refs):
    base_ref, out_ref = refs[-2:]
    rows, wide = out_ref.shape
    total, crossed = fold(refs[:-2])
    out_ref[:, 0 : wide - LANES] = total.astype(BF16)
    loss = base_ref[:, 0:1] - crossed
    out_ref[:, wide - LANES : wide] = lanes_of(pieces(loss), rows).astype(BF16)


def whole(shape):
    return pl.BlockSpec(shape, lambda *_: (0,) * len(shape))


def shifted(value, ring, along_x, step):
    count = lax.axis_size("ctx")
    lines = count // ring
    pairs = []
    for x in range(lines):
        for z in range(ring):
            to = (x + step) % lines * ring + z if along_x else x * ring + (z + step) % ring
            pairs.append((x * ring + z, to))
    return lax.ppermute(value, "ctx", pairs)


def spread(value, ring, along_x):
    count = lax.axis_size("ctx") // ring if along_x else ring
    return [value] + [shifted(value, ring, along_x, step) for step in range(1, count)]


def exchange(
    capacity, ring, head_weight, incoming, compact_slot, whole_slot, own_slot, place, behind, *lines
):
    ctx_count = lax.axis_size("ctx")
    voc_count, held, part, _ = incoming.shape
    width, cols = head_weight.shape
    dev_blocks = cols // LANES
    owned_blocks = voc_count * dev_blocks
    rows = ctx_count * part
    slots = ctx_count * capacity
    wide = width + LANES
    smem = pl.BlockSpec(memory_space=pltpu.SMEM)

    weights = lax.all_gather(head_weight, "voc", axis=0, tiled=False)
    slot = compact_slot if capacity == COMPACT else whole_slot
    target, mass = pl.pallas_call(
        collect_kernel,
        out_shape=(
            jax.ShapeDtypeStruct((slots, part, LANES), BF16),
            jax.ShapeDtypeStruct((part, LANES), F32),
        ),
        in_specs=[smem, pl.BlockSpec(memory_space=pltpu.VMEM)],
        scratch_shapes=[
            pltpu.VMEM((slots, part, LANES), F32),
            pltpu.VMEM((voc_count, part, LANES), F32),
        ],
        compiler_params=params(20),
        cost_estimate=pl.CostEstimate(
            flops=4 * slots * part * LANES, bytes_accessed=6 * 1024 * 1024, transcendentals=0
        ),
        name="collect_targets",
    )(slot, incoming)
    target = target.reshape(ctx_count, capacity, part, LANES)
    arrived = lax.all_to_all(target, "ctx", 0, 0, tiled=True)
    hidden_rows = pl.pallas_call(
        arrange_kernel,
        out_shape=jax.ShapeDtypeStruct((ctx_count, part, wide), BF16),
        in_specs=[smem] + [pl.BlockSpec(memory_space=pltpu.VMEM)] * len(lines),
        scratch_shapes=[pltpu.VMEM((ctx_count, part, wide), BF16)],
        compiler_params=params(),
        name="arrange_rows",
    )(behind, *[line.reshape(ring, part, wide) for line in lines]).reshape(rows, wide)
    hidden_t = hidden_rows[:, :width].T

    logits, stats = pl.pallas_call(
        logits_kernel,
        grid=(voc_count,),
        in_specs=[
            pl.BlockSpec((rows, width), lambda j: (0, 0)),
            pl.BlockSpec((1, width, cols), lambda j: (j, 0, 0)),
            whole((part, LANES)),
        ],
        out_specs=(
            pl.BlockSpec((1, rows, cols), lambda j: (j, 0, 0)),
            whole((ctx_count, 4, rows)),
        ),
        out_shape=(
            jax.ShapeDtypeStruct((voc_count, rows, cols), F32),
            jax.ShapeDtypeStruct((ctx_count, 4, rows), F32),
        ),
        scratch_shapes=[pltpu.VMEM((rows, LANES), F32)] * 2,
        compiler_params=params(16),
        cost_estimate=pl.CostEstimate(
            flops=2 * rows * width * cols * voc_count,
            bytes_accessed=18 * 1024 * 1024,
            transcendentals=rows * cols * voc_count,
        ),
        name="student_logits",
    )(hidden_rows, weights, mass)
    all_stats = lax.all_to_all(stats, "ctx", 0, 0, tiled=True)

    dweight, dhidden, base = pl.pallas_call(
        grad_kernel,
        grid=(voc_count,),
        in_specs=[
            smem,
            smem,
            whole((ctx_count, 4, rows)),
            pl.BlockSpec((1, rows, cols), lambda j: (j, 0, 0)),
            whole((ctx_count, capacity, part, LANES)),
            whole((rows, width + LANES)),
            whole((width, rows)),
            pl.BlockSpec((1, width, cols), lambda j: (j, 0, 0)),
        ],
        out_specs=(
            pl.BlockSpec((1, width, cols), lambda j: (j, 0, 0)),
            whole((ctx_count, part, width + LANES)),
            whole((part, LANES)),
        ),
        out_shape=(
            jax.ShapeDtypeStruct((voc_count, width, cols), BF16),
            jax.ShapeDtypeStruct((ctx_count, part, width + LANES), BF16),
            jax.ShapeDtypeStruct((part, LANES), F32),
        ),
        scratch_shapes=[pltpu.VMEM((rows, LANES), F32)] * 4 + [pltpu.VMEM((rows, width), F32)],
        compiler_params=params(56),
        cost_estimate=pl.CostEstimate(
            flops=4 * rows * width * cols * voc_count,
            bytes_accessed=30 * 1024 * 1024,
            transcendentals=rows * cols * voc_count,
        ),
        name="grads",
    )(place, own_slot, all_stats, logits, arrived, hidden_rows, hidden_t, weights)
    return dweight, dhidden, base


def local(hidden, token_weight, head_weight, teacher_logits, block_coeff, block_map):
    ctx_count = lax.axis_size("ctx")
    voc_count = lax.axis_size("voc")
    voc_index = lax.axis_index("voc")
    ctx_index = lax.axis_index("ctx")
    rows_dev, width = hidden.shape
    half_rows = rows_dev // 2
    part = rows_dev // voc_count
    half_groups = voc_count // 2
    local_blocks = block_coeff.shape[0]
    cols = head_weight.shape[1]
    dev_blocks = cols // LANES
    owned_blocks = voc_count * dev_blocks
    slots = ctx_count * owned_blocks
    rows = ctx_count * part
    wide = width + LANES

    parity = voc_index // half_groups
    fold_side = jnp.where(ctx_index % 2 == parity, 0, 1)
    start = fold_side * half_rows + voc_index % half_groups * part
    mine = lax.dynamic_slice_in_dim(hidden, start, part, 0)
    mine_weight = lax.dynamic_slice_in_dim(token_weight, start, part, 0)
    mine = jnp.concatenate([mine, jnp.broadcast_to(mine_weight[:, None], (part, LANES))], axis=1)
    ring = min(8, ctx_count)
    outgoing = pl.pallas_call(
        teacher_kernel,
        out_shape=jax.ShapeDtypeStruct((voc_count, local_blocks + 1, part, LANES), BF16),
        compiler_params=params(56),
        cost_estimate=pl.CostEstimate(
            flops=2 * rows_dev * local_blocks * LANES * LANES,
            bytes_accessed=6 * 1024 * 1024,
            transcendentals=rows_dev * local_blocks * LANES,
        ),
        name="teacher_map",
    )(teacher_logits, block_coeff)
    outgoing, mine = lax.optimization_barrier((outgoing, mine))
    near = pl.pallas_call(
        stack_kernel,
        out_shape=jax.ShapeDtypeStruct((ring * part, wide), BF16),
        compiler_params=params(),
        name="stack_rows",
    )(*spread(mine, ring, False))
    incoming = lax.all_to_all(outgoing, "voc", 0, 0, tiled=True)

    wanted = jnp.any(
        block_map[:, None] == jnp.arange(slots, dtype=jnp.int32)[None, :], axis=0
    ).astype(jnp.int32).reshape(ctx_count, owned_blocks)
    number = jnp.cumsum(wanted, axis=1) - wanted
    fits = jnp.max(jnp.sum(wanted, axis=1)) <= COMPACT
    own_slot = jnp.where(wanted == 1, number, -1)
    own_slot = lax.dynamic_index_in_dim(own_slot, ctx_index, 0, keepdims=False)
    in_order = number.reshape(slots)[block_map]
    compact_slot = block_map // owned_blocks * COMPACT + in_order
    whole_slot = block_map // owned_blocks * owned_blocks + in_order

    source = jnp.arange(ctx_count, dtype=jnp.int32)
    half_block = 2 * source + parity
    place = jnp.where(half_block < ctx_count, half_block, 2 * ctx_count - 1 - half_block)
    own_half = jnp.where(fold_side == 0, ctx_index, 2 * ctx_count - 1 - ctx_index)
    behind = (ctx_index // ring - place // ring) % (ctx_count // ring) * ring + (ctx_index - place) % ring
    ahead = (place // ring - ctx_index // ring) % (ctx_count // ring) * ring + (place - ctx_index) % ring
    place = jnp.concatenate([ahead, (own_half // 2)[None]]).astype(jnp.int32)
    lines = spread(near, ring, True)
    operands = lax.optimization_barrier(
        (incoming, compact_slot, whole_slot, own_slot, place, behind, *lines)
    )
    dweight, dhidden, base = lax.cond(
        fits,
        functools.partial(exchange, COMPACT, ring),
        functools.partial(exchange, owned_blocks, ring),
        head_weight,
        *operands,
    )
    grad_weight = lax.psum_scatter(dweight, "voc", scatter_dimension=0, tiled=True)
    grad_weight = grad_weight.reshape(width, cols).astype(F32)
    pieces_x = dhidden.reshape(ctx_count // ring, ring * part, wide)
    parts = [pieces_x[0]]
    parts += [shifted(pieces_x[e], ring, True, e) for e in range(1, ctx_count // ring)]
    folded = pl.pallas_call(
        fold_kernel,
        out_shape=jax.ShapeDtypeStruct((ring * part, wide), BF16),
        compiler_params=params(),
        name="fold_rows",
    )(*parts)
    pieces_z = folded.reshape(ring, part, wide)
    parts = [pieces_z[0]] + [shifted(pieces_z[e], ring, False, e) for e in range(1, ring)]
    done = pl.pallas_call(
        finish_kernel,
        out_shape=jax.ShapeDtypeStruct((part, wide), BF16),
        compiler_params=params(),
        name="finish_rows",
    )(*parts, base)
    all_done = lax.all_gather(done, "voc", axis=0, tiled=False)
    turned = (ctx_index % 2 * half_groups).astype(jnp.int32)
    grad_hidden, loss_tile = pl.pallas_call(
        rows_kernel,
        in_specs=[
            pl.BlockSpec(memory_space=pltpu.SMEM),
            pl.BlockSpec(memory_space=pltpu.VMEM),
        ],
        out_shape=(
            jax.ShapeDtypeStruct((rows_dev, width), BF16),
            jax.ShapeDtypeStruct((rows_dev, LANES), F32),
        ),
        compiler_params=params(),
        name="own_rows",
    )(turned[None], all_done)
    row_loss = loss_tile[:, 0]
    return (grad_hidden, grad_weight, row_loss)


def solution(mesh):
    return jax.shard_map(
        local,
        mesh=mesh,
        in_specs=(
            P("ctx", None),
            P("ctx"),
            P(None, ("ctx", "voc")),
            P("ctx", "voc"),
            P("voc", None, None),
            P(),
        ),
        out_specs=(P("ctx", None), P(None, ("ctx", "voc")), P("ctx")),
        check_vma=False,
    )
```

```python
import functools

import jax
import jax.numpy as jnp
from jax import lax
from jax.experimental import pallas as pl
from jax.experimental.pallas import tpu as pltpu
from jax.sharding import PartitionSpec as P

F32 = jnp.float32
BF16 = jnp.bfloat16
LANES = 128
COMPACT = 20
MIB = 1024 * 1024


def params(mib=8):
    return pltpu.CompilerParams(vmem_limit_bytes=mib * MIB)


def pieces(value):
    high = value.astype(BF16).astype(F32)
    rest = value - high
    middle = rest.astype(BF16).astype(F32)
    return high, middle, rest - middle


def lanes_of(columns, rows):
    lane = lax.broadcasted_iota(jnp.int32, (rows, LANES), 1)
    tile = jnp.zeros((rows, LANES), F32)
    for index, column in enumerate(columns):
        tile = jnp.where(lane == index, column, tile)
    return tile


def teacher_kernel(logits_ref, coeff_ref, out_ref):
    rows = logits_ref.shape[0]
    groups, _, part, _ = out_ref.shape
    blocks = coeff_ref.shape[0]

    def top(b, carry):
        return jnp.maximum(carry, logits_ref[:, pl.ds(pl.multiple_of(b * LANES, LANES), LANES)])

    widest = lax.fori_loop(
        1, blocks, top, logits_ref[:, 0:LANES], unroll=4
    ).astype(F32)
    row_max = jnp.max(widest, axis=1, keepdims=True)

    def one(b, total):
        x = logits_ref[:, pl.ds(pl.multiple_of(b * LANES, LANES), LANES)].astype(F32)
        e = jnp.exp(x - row_max)
        mapped = jnp.dot(e.astype(BF16), coeff_ref[b], preferred_element_type=F32).astype(BF16)
        out_ref[:, b] = mapped.reshape(groups, part, LANES)
        return total + e

    total = lax.fori_loop(0, blocks, one, jnp.zeros((rows, LANES), F32), unroll=4)
    row_total = jnp.sum(total, axis=1, keepdims=True)
    tile = lanes_of((row_max,) + pieces(row_total), rows).astype(BF16)
    out_ref[:, blocks] = tile.reshape(groups, part, LANES)


def collect_kernel(slot_ref, in_ref, out_ref, mass_ref, sums, scales):
    voc_count, held, part, _ = in_ref.shape
    blocks = held - 1
    slots = out_ref.shape[0]
    tops, totals = [], []
    for v in range(voc_count):
        tile = in_ref[v, blocks].astype(F32)
        tops.append(tile[:, 0:1])
        totals.append(tile[:, 1:2] + tile[:, 2:3] + tile[:, 3:4])
    top = functools.reduce(jnp.maximum, tops)
    total = functools.reduce(
        jnp.add, [part_total * jnp.exp(part_top - top) for part_total, part_top in zip(totals, tops)]
    )
    for v in range(voc_count):
        scales[v] = jnp.broadcast_to(jnp.exp(tops[v] - top) / total, (part, LANES))

    def clear(s, carry):
        sums[s] = jnp.zeros((part, LANES), F32)
        return carry

    lax.fori_loop(0, slots, clear, 0, unroll=8)
    for v in range(voc_count):
        scale = scales[v]

        def add(b, carry):
            slot = slot_ref[v * blocks + b]
            sums[slot] = sums[slot] + scale * in_ref[v, b].astype(F32)
            return carry

        lax.fori_loop(0, blocks, add, 0, unroll=4)

    def store(s, mass):
        target = sums[s].astype(BF16)
        out_ref[s] = target
        return mass + target.astype(F32)

    mass = lax.fori_loop(0, slots, store, jnp.zeros((part, LANES), F32), unroll=8)
    mass_ref[...] = jnp.broadcast_to(jnp.sum(mass, axis=1, keepdims=True), (part, LANES))


def logits_kernel(hidden_ref, weight_ref, mass_ref, logits_ref, stats_ref, tops, totals):
    step = pl.program_id(0)
    rows, cols = logits_ref.shape[1:]

    @pl.when(step == 0)
    def _():
        tops[...] = jnp.full(tops.shape, -jnp.inf, F32)
        totals[...] = jnp.zeros(totals.shape, F32)

    logits = jnp.dot(hidden_ref[...], weight_ref[0], preferred_element_type=F32)
    logits_ref[0] = logits
    tiles = [logits[:, k : k + LANES] for k in range(0, cols, LANES)]
    old = tops[...]
    new = functools.reduce(jnp.maximum, tiles, old)
    total = totals[...] * jnp.exp(old - new)
    for tile in tiles:
        total = total + jnp.exp(tile - new)
    tops[...] = new
    totals[...] = total

    @pl.when(step == pl.num_programs(0) - 1)
    def _():
        lane_top, lane_total = tops[...], totals[...]
        top = jnp.max(lane_top, axis=1, keepdims=True)
        total = jnp.sum(lane_total * jnp.exp(lane_top - top), axis=1, keepdims=True)
        part = mass_ref.shape[0]
        flat = jnp.transpose(lanes_of((top, total), rows))
        mass = jnp.transpose(mass_ref[...])
        mass = jnp.concatenate([mass[0:1], jnp.zeros((1, rows - part), F32)], axis=1)
        packed = jnp.concatenate([flat[0:2], mass, jnp.zeros((1, rows), F32)], axis=0)
        stats_ref[...] = jnp.concatenate([packed, jnp.zeros((4, rows), F32)], axis=0)


def grad_kernel(
    place_ref, slot_ref, from_ref, stats_refs, logits_ref, target_ref, hidden_ref, hidden_t_ref, weight_ref,
    dweight_ref, dhidden_ref, base_ref, norm, mass, gain, cross, partial, by_place, in_order,
):
    step = pl.program_id(0)
    count, _, part, _ = target_ref.shape
    rows, cols = logits_ref.shape[1:]
    width = weight_ref.shape[1]

    @pl.when(step == 0)
    def _():
        top = functools.reduce(jnp.maximum, [ref[0:1] for ref in stats_refs])
        total = functools.reduce(
            jnp.add, [ref[1:2] * jnp.exp(ref[0:1] - top) for ref in stats_refs]
        )
        norm[...] = jnp.transpose(jnp.broadcast_to(top + jnp.log(total), (LANES, rows)))
        ring = stats_refs[0].shape[0] - 8
        for e, ref in enumerate(stats_refs):
            for k in range(ring):
                by_place[e * ring + k] = ref[8 + k : 9 + k, 0:LANES]
        for t in range(count):
            in_order[t] = by_place[from_ref[t]]
        own = in_order[...][:, 0, :]
        spread = jnp.broadcast_to(own[:, None, :], (count, part, LANES))
        diagonal = lax.broadcasted_iota(jnp.int32, (count, part, LANES), 1) == lax.broadcasted_iota(
            jnp.int32, (count, part, LANES), 2
        )
        column = jnp.sum(jnp.where(diagonal, spread, 0.0), axis=2, keepdims=True).reshape(rows, 1)
        mass[...] = jnp.broadcast_to(column, (rows, LANES))
        gain[...] = jnp.broadcast_to(
            hidden_ref[:, width : width + LANES].astype(F32)[:, 0:1], (rows, LANES)
        )
        cross[...] = jnp.zeros(cross.shape, F32)

    norm_tile, mass_tile, gain_tile = norm[...], mass[...], gain[...]
    crossed = cross[...]
    grads = []
    for q in range(cols // LANES):
        logit = logits_ref[0, :, q * LANES : (q + 1) * LANES]
        slot = slot_ref[step * (cols // LANES) + q]
        held = target_ref[:, jnp.maximum(slot, 0)].reshape(rows, LANES).astype(F32)
        target = jnp.where(slot >= 0, held, 0.0)
        crossed = crossed + target * logit
        grads.append(
            (gain_tile * (mass_tile * jnp.exp(logit - norm_tile) - target)).astype(BF16)
        )
    cross[...] = crossed
    grad = jnp.concatenate(grads, axis=1)
    dweight_ref[0] = jnp.dot(hidden_t_ref[...], grad, preferred_element_type=F32).astype(BF16)
    product = lax.dot_general(
        grad, weight_ref[0], (((1,), (1,)), ((), ())), preferred_element_type=F32
    )

    @pl.when(step == 0)
    def _():
        partial[...] = product

    @pl.when(step > 0)
    def _():
        partial[...] = partial[...] + product

    @pl.when(step == pl.num_programs(0) - 1)
    def _():
        cross_sum = jnp.sum(cross[...], axis=1, keepdims=True)
        cross[...] = lanes_of(pieces(cross_sum), rows)
        for t in range(count):
            c = place_ref[t]
            dhidden_ref[c, :, 0:width] = partial[t * part : (t + 1) * part, :].astype(BF16)
            dhidden_ref[c, :, width : width + LANES] = cross[t * part : (t + 1) * part, :].astype(BF16)
        mass[...] = mass[...] * norm[...]
        start = pl.multiple_of(place_ref[count] * part, part)
        base_ref[...] = mass[pl.ds(start, part), :]


def grads_of(lines):
    def kernel(place_ref, slot_ref, from_ref, *refs):
        grad_kernel(place_ref, slot_ref, from_ref, refs[:lines], *refs[lines:])

    return kernel


def merge_kernel(*refs):
    out_ref = refs[-1]
    top = functools.reduce(jnp.maximum, [ref[0:1] for ref in refs[:-1]])
    total = functools.reduce(jnp.add, [ref[1:2] * jnp.exp(ref[0:1] - top) for ref in refs[:-1]])
    out_ref[0:8] = jnp.concatenate([top, total, jnp.zeros((6, top.shape[1]), F32)], axis=0)
    for k, ref in enumerate(refs[:-1]):
        out_ref[8 + k : 9 + k] = ref[2:3]


def rows_kernel(turned_ref, in_ref, rows_ref, loss_ref):
    count, part, wide = in_ref.shape
    width = wide - LANES
    for v in range(count):
        got = in_ref[(v + turned_ref[0]) % count]
        rows_ref[v * part : (v + 1) * part, :] = got[:, 0:width]
        tail = got[:, width:wide].astype(F32)
        loss_ref[v * part : (v + 1) * part, :] = jnp.broadcast_to(
            tail[:, 0:1] + tail[:, 1:2] + tail[:, 2:3], (part, LANES)
        )


def stack_kernel(*refs):
    out_ref = refs[-1]
    part = refs[0].shape[0]
    for k, ref in enumerate(refs[:-1]):
        out_ref[k * part : (k + 1) * part, :] = ref[...]


def arrange_kernel(behind_ref, *refs):
    out_ref, held = refs[-2:]
    near = refs[0].shape[0]
    for k, ref in enumerate(refs[:-2]):
        held[k * near : (k + 1) * near] = ref[...]
    for t in range(out_ref.shape[0]):
        out_ref[t] = held[behind_ref[t]]


def fold(refs):
    wide = refs[0].shape[-1]
    total = refs[0][...].astype(F32)
    for ref in refs[1:]:
        total = total + ref[...].astype(F32)
    tail = total[:, wide - LANES :]
    return total[:, : wide - LANES], tail[:, 0:1] + tail[:, 1:2] + tail[:, 2:3]


def fold_kernel(*refs):
    out_ref = refs[-1]
    rows, wide = out_ref.shape
    total, crossed = fold(refs[:-1])
    out_ref[:, 0 : wide - LANES] = total.astype(BF16)
    out_ref[:, wide - LANES : wide] = lanes_of(pieces(crossed), rows).astype(BF16)


def finish_kernel(*refs):
    base_ref, out_ref = refs[-2:]
    rows, wide = out_ref.shape
    total, crossed = fold(refs[:-2])
    out_ref[:, 0 : wide - LANES] = total.astype(BF16)
    loss = base_ref[:, 0:1] - crossed
    out_ref[:, wide - LANES : wide] = lanes_of(pieces(loss), rows).astype(BF16)


def whole(shape):
    return pl.BlockSpec(shape, lambda *_: (0,) * len(shape))


def shifted(value, ring, along_x, step):
    count = lax.axis_size("ctx")
    lines = count // ring
    pairs = []
    for x in range(lines):
        for z in range(ring):
            to = (x + step) % lines * ring + z if along_x else x * ring + (z + step) % ring
            pairs.append((x * ring + z, to))
    return lax.ppermute(value, "ctx", pairs)


def spread(value, ring, along_x):
    count = lax.axis_size("ctx") // ring if along_x else ring
    return [value] + [shifted(value, ring, along_x, step) for step in range(1, count)]


def exchange(
    capacity, ring, head_weight, incoming, compact_slot, whole_slot, own_slot, place, behind, from_where, *lines
):
    ctx_count = lax.axis_size("ctx")
    voc_count, held, part, _ = incoming.shape
    width, cols = head_weight.shape
    dev_blocks = cols // LANES
    owned_blocks = voc_count * dev_blocks
    rows = ctx_count * part
    slots = ctx_count * capacity
    wide = width + LANES
    smem = pl.BlockSpec(memory_space=pltpu.SMEM)

    weights = lax.all_gather(head_weight, "voc", axis=0, tiled=False)
    slot = compact_slot if capacity == COMPACT else whole_slot
    target, mass = pl.pallas_call(
        collect_kernel,
        out_shape=(
            jax.ShapeDtypeStruct((slots, part, LANES), BF16),
            jax.ShapeDtypeStruct((part, LANES), F32),
        ),
        in_specs=[smem, pl.BlockSpec(memory_space=pltpu.VMEM)],
        scratch_shapes=[
            pltpu.VMEM((slots, part, LANES), F32),
            pltpu.VMEM((voc_count, part, LANES), F32),
        ],
        compiler_params=params(20),
        cost_estimate=pl.CostEstimate(
            flops=4 * slots * part * LANES, bytes_accessed=6 * 1024 * 1024, transcendentals=0
        ),
        name="collect_targets",
    )(slot, incoming)
    target = target.reshape(ctx_count, capacity, part, LANES)
    arrived = lax.all_to_all(target, "ctx", 0, 0, tiled=True)
    hidden_rows = pl.pallas_call(
        arrange_kernel,
        out_shape=jax.ShapeDtypeStruct((ctx_count, part, wide), BF16),
        in_specs=[smem] + [pl.BlockSpec(memory_space=pltpu.VMEM)] * len(lines),
        scratch_shapes=[pltpu.VMEM((ctx_count, part, wide), BF16)],
        compiler_params=params(),
        name="arrange_rows",
    )(behind, *[line.reshape(ring, part, wide) for line in lines]).reshape(rows, wide)
    hidden_t = hidden_rows[:, :width].T

    logits, stats = pl.pallas_call(
        logits_kernel,
        grid=(voc_count,),
        in_specs=[
            pl.BlockSpec((rows, width), lambda j: (0, 0)),
            pl.BlockSpec((1, width, cols), lambda j: (j, 0, 0)),
            whole((part, LANES)),
        ],
        out_specs=(
            pl.BlockSpec((1, rows, cols), lambda j: (j, 0, 0)),
            whole((8, rows)),
        ),
        out_shape=(
            jax.ShapeDtypeStruct((voc_count, rows, cols), F32),
            jax.ShapeDtypeStruct((8, rows), F32),
        ),
        scratch_shapes=[pltpu.VMEM((rows, LANES), F32)] * 2,
        compiler_params=params(16),
        cost_estimate=pl.CostEstimate(
            flops=2 * rows * width * cols * voc_count,
            bytes_accessed=18 * 1024 * 1024,
            transcendentals=rows * cols * voc_count,
        ),
        name="student_logits",
    )(hidden_rows, weights, mass)
    def merge(parts):
        return pl.pallas_call(
            merge_kernel,
            out_shape=jax.ShapeDtypeStruct((8 + ring, rows), F32),
            compiler_params=params(),
            name="merge_stats",
        )(*parts)

    if capacity == COMPACT:
        all_stats = spread(merge(spread(stats, ring, False)), ring, True)
    else:
        arrived, stats = lax.optimization_barrier((arrived, stats))
        everywhere = jnp.broadcast_to(stats[None], (ctx_count, 8, rows))
        got = lax.all_to_all(everywhere, "ctx", 0, 0, tiled=True)
        all_stats = [
            merge([got[e + k] for k in range(ring)]) for e in range(0, ctx_count, ring)
        ]
        from_where = jnp.arange(ctx_count, dtype=jnp.int32)

    dweight, dhidden, base = pl.pallas_call(
        grads_of(len(all_stats)),
        grid=(voc_count,),
        in_specs=[
            smem,
            smem,
            smem,
        ]
        + [whole((8 + ring, rows))] * len(all_stats)
        + [
            pl.BlockSpec((1, rows, cols), lambda j: (j, 0, 0)),
            whole((ctx_count, capacity, part, LANES)),
            whole((rows, width + LANES)),
            whole((width, rows)),
            pl.BlockSpec((1, width, cols), lambda j: (j, 0, 0)),
        ],
        out_specs=(
            pl.BlockSpec((1, width, cols), lambda j: (j, 0, 0)),
            whole((ctx_count, part, width + LANES)),
            whole((part, LANES)),
        ),
        out_shape=(
            jax.ShapeDtypeStruct((voc_count, width, cols), BF16),
            jax.ShapeDtypeStruct((ctx_count, part, width + LANES), BF16),
            jax.ShapeDtypeStruct((part, LANES), F32),
        ),
        scratch_shapes=[pltpu.VMEM((rows, LANES), F32)] * 4
        + [pltpu.VMEM((rows, width), F32)]
        + [pltpu.VMEM((ctx_count, 1, LANES), F32)] * 2,
        compiler_params=params(56),
        cost_estimate=pl.CostEstimate(
            flops=4 * rows * width * cols * voc_count,
            bytes_accessed=30 * 1024 * 1024,
            transcendentals=rows * cols * voc_count,
        ),
        name="grads",
    )(place, own_slot, from_where, *all_stats, logits, arrived, hidden_rows, hidden_t, weights)
    return dweight, dhidden, base


def local(hidden, token_weight, head_weight, teacher_logits, block_coeff, block_map):
    ctx_count = lax.axis_size("ctx")
    voc_count = lax.axis_size("voc")
    voc_index = lax.axis_index("voc")
    ctx_index = lax.axis_index("ctx")
    rows_dev, width = hidden.shape
    half_rows = rows_dev // 2
    part = rows_dev // voc_count
    half_groups = voc_count // 2
    local_blocks = block_coeff.shape[0]
    cols = head_weight.shape[1]
    dev_blocks = cols // LANES
    owned_blocks = voc_count * dev_blocks
    slots = ctx_count * owned_blocks
    rows = ctx_count * part
    wide = width + LANES

    parity = voc_index // half_groups
    fold_side = jnp.where(ctx_index % 2 == parity, 0, 1)
    start = fold_side * half_rows + voc_index % half_groups * part
    mine = lax.dynamic_slice_in_dim(hidden, start, part, 0)
    mine_weight = lax.dynamic_slice_in_dim(token_weight, start, part, 0)
    mine = jnp.concatenate([mine, jnp.broadcast_to(mine_weight[:, None], (part, LANES))], axis=1)
    ring = min(8, ctx_count)
    outgoing = pl.pallas_call(
        teacher_kernel,
        out_shape=jax.ShapeDtypeStruct((voc_count, local_blocks + 1, part, LANES), BF16),
        compiler_params=params(56),
        cost_estimate=pl.CostEstimate(
            flops=2 * rows_dev * local_blocks * LANES * LANES,
            bytes_accessed=6 * 1024 * 1024,
            transcendentals=rows_dev * local_blocks * LANES,
        ),
        name="teacher_map",
    )(teacher_logits, block_coeff)
    outgoing, mine = lax.optimization_barrier((outgoing, mine))
    near = pl.pallas_call(
        stack_kernel,
        out_shape=jax.ShapeDtypeStruct((ring * part, wide), BF16),
        compiler_params=params(),
        name="stack_rows",
    )(*spread(mine, ring, False))
    incoming = lax.all_to_all(outgoing, "voc", 0, 0, tiled=True)

    wanted = jnp.any(
        block_map[:, None] == jnp.arange(slots, dtype=jnp.int32)[None, :], axis=0
    ).astype(jnp.int32).reshape(ctx_count, owned_blocks)
    number = jnp.cumsum(wanted, axis=1) - wanted
    fits = jnp.max(jnp.sum(wanted, axis=1)) <= COMPACT
    own_slot = jnp.where(wanted == 1, number, -1)
    own_slot = lax.dynamic_index_in_dim(own_slot, ctx_index, 0, keepdims=False)
    in_order = number.reshape(slots)[block_map]
    compact_slot = block_map // owned_blocks * COMPACT + in_order
    whole_slot = block_map // owned_blocks * owned_blocks + in_order

    source = jnp.arange(ctx_count, dtype=jnp.int32)
    half_block = 2 * source + parity
    place = jnp.where(half_block < ctx_count, half_block, 2 * ctx_count - 1 - half_block)
    own_half = jnp.where(fold_side == 0, ctx_index, 2 * ctx_count - 1 - ctx_index)
    behind = (ctx_index // ring - place // ring) % (ctx_count // ring) * ring + (ctx_index - place) % ring
    from_where = (ctx_index // ring - source // ring) % (ctx_count // ring) * ring + (
        ctx_index - source
    ) % ring
    ahead = (place // ring - ctx_index // ring) % (ctx_count // ring) * ring + (place - ctx_index) % ring
    place = jnp.concatenate([ahead, (own_half // 2)[None]]).astype(jnp.int32)
    lines = spread(near, ring, True)
    operands = lax.optimization_barrier(
        (incoming, compact_slot, whole_slot, own_slot, place, behind, from_where, *lines)
    )
    dweight, dhidden, base = lax.cond(
        fits,
        functools.partial(exchange, COMPACT, ring),
        functools.partial(exchange, owned_blocks, ring),
        head_weight,
        *operands,
    )
    grad_weight = lax.psum_scatter(dweight, "voc", scatter_dimension=0, tiled=True)
    grad_weight = grad_weight.reshape(width, cols).astype(F32)
    pieces_x = dhidden.reshape(ctx_count // ring, ring * part, wide)
    parts = [pieces_x[0]]
    parts += [shifted(pieces_x[e], ring, True, e) for e in range(1, ctx_count // ring)]
    folded = pl.pallas_call(
        fold_kernel,
        out_shape=jax.ShapeDtypeStruct((ring * part, wide), BF16),
        compiler_params=params(),
        name="fold_rows",
    )(*parts)
    pieces_z = folded.reshape(ring, part, wide)
    parts = [pieces_z[0]] + [shifted(pieces_z[e], ring, False, e) for e in range(1, ring)]
    done = pl.pallas_call(
        finish_kernel,
        out_shape=jax.ShapeDtypeStruct((part, wide), BF16),
        compiler_params=params(),
        name="finish_rows",
    )(*parts, base)
    all_done = lax.all_gather(done, "voc", axis=0, tiled=False)
    turned = (ctx_index % 2 * half_groups).astype(jnp.int32)
    grad_hidden, loss_tile = pl.pallas_call(
        rows_kernel,
        in_specs=[
            pl.BlockSpec(memory_space=pltpu.SMEM),
            pl.BlockSpec(memory_space=pltpu.VMEM),
        ],
        out_shape=(
            jax.ShapeDtypeStruct((rows_dev, width), BF16),
            jax.ShapeDtypeStruct((rows_dev, LANES), F32),
        ),
        compiler_params=params(),
        name="own_rows",
    )(turned[None], all_done)
    row_loss = loss_tile[:, 0]
    return (grad_hidden, grad_weight, row_loss)


def solution(mesh):
    return jax.shard_map(
        local,
        mesh=mesh,
        in_specs=(
            P("ctx", None),
            P("ctx"),
            P(None, ("ctx", "voc")),
            P("ctx", "voc"),
            P("voc", None, None),
            P(),
        ),
        out_specs=(P("ctx", None), P(None, ("ctx", "voc")), P("ctx")),
        check_vma=False,
    )
```

```python
import functools

import jax
import jax.numpy as jnp
from jax import lax
from jax.experimental import pallas as pl
from jax.experimental.pallas import tpu as pltpu
from jax.sharding import PartitionSpec as P

F32 = jnp.float32
BF16 = jnp.bfloat16
LANES = 128
COMPACT = 20
MIB = 1024 * 1024


def params(mib=8):
    return pltpu.CompilerParams(vmem_limit_bytes=mib * MIB)


def pieces(value):
    high = value.astype(BF16).astype(F32)
    rest = value - high
    middle = rest.astype(BF16).astype(F32)
    return high, middle, rest - middle


def lanes_of(columns, rows):
    lane = lax.broadcasted_iota(jnp.int32, (rows, LANES), 1)
    tile = jnp.zeros((rows, LANES), F32)
    for index, column in enumerate(columns):
        tile = jnp.where(lane == index, column, tile)
    return tile


def teacher_kernel(logits_ref, coeff_ref, out_ref):
    rows = logits_ref.shape[0]
    groups, _, part, _ = out_ref.shape
    blocks = coeff_ref.shape[0]

    def top(b, carry):
        return jnp.maximum(carry, logits_ref[:, pl.ds(pl.multiple_of(b * LANES, LANES), LANES)])

    widest = lax.fori_loop(
        1, blocks, top, logits_ref[:, 0:LANES], unroll=4
    ).astype(F32)
    row_max = jnp.max(widest, axis=1, keepdims=True)

    def one(b, total):
        x = logits_ref[:, pl.ds(pl.multiple_of(b * LANES, LANES), LANES)].astype(F32)
        e = jnp.exp(x - row_max)
        mapped = jnp.dot(e.astype(BF16), coeff_ref[b], preferred_element_type=F32).astype(BF16)
        out_ref[:, b] = mapped.reshape(groups, part, LANES)
        return total + e

    total = lax.fori_loop(0, blocks, one, jnp.zeros((rows, LANES), F32), unroll=4)
    row_total = jnp.sum(total, axis=1, keepdims=True)
    tile = lanes_of((row_max,) + pieces(row_total), rows).astype(BF16)
    out_ref[:, blocks] = tile.reshape(groups, part, LANES)


def collect_kernel(slot_ref, in_ref, out_ref, mass_ref, sums, scales):
    voc_count, held, part, _ = in_ref.shape
    blocks = held - 1
    slots = out_ref.shape[0]
    tops, totals = [], []
    for v in range(voc_count):
        tile = in_ref[v, blocks].astype(F32)
        tops.append(tile[:, 0:1])
        totals.append(tile[:, 1:2] + tile[:, 2:3] + tile[:, 3:4])
    top = functools.reduce(jnp.maximum, tops)
    total = functools.reduce(
        jnp.add, [part_total * jnp.exp(part_top - top) for part_total, part_top in zip(totals, tops)]
    )
    for v in range(voc_count):
        scales[v] = jnp.broadcast_to(jnp.exp(tops[v] - top) / total, (part, LANES))

    def clear(s, carry):
        sums[s] = jnp.zeros((part, LANES), F32)
        return carry

    lax.fori_loop(0, slots, clear, 0, unroll=8)
    for v in range(voc_count):
        scale = scales[v]

        def add(b, carry):
            slot = slot_ref[v * blocks + b]
            sums[slot] = sums[slot] + scale * in_ref[v, b].astype(F32)
            return carry

        lax.fori_loop(0, blocks, add, 0, unroll=4)

    def store(s, mass):
        target = sums[s].astype(BF16)
        out_ref[s] = target
        return mass + target.astype(F32)

    mass = lax.fori_loop(0, slots, store, jnp.zeros((part, LANES), F32), unroll=8)
    mass_ref[...] = jnp.broadcast_to(jnp.sum(mass, axis=1, keepdims=True), (part, LANES))


def logits_kernel(hidden_ref, weight_ref, mass_ref, logits_ref, stats_ref, tops, totals):
    step = pl.program_id(0)
    rows, cols = logits_ref.shape[1:]

    @pl.when(step == 0)
    def _():
        tops[...] = jnp.full(tops.shape, -jnp.inf, F32)
        totals[...] = jnp.zeros(totals.shape, F32)

    logits = jnp.dot(hidden_ref[...], weight_ref[0], preferred_element_type=F32)
    logits_ref[0] = logits
    tiles = [logits[:, k : k + LANES] for k in range(0, cols, LANES)]
    old = tops[...]
    new = functools.reduce(jnp.maximum, tiles, old)
    total = totals[...] * jnp.exp(old - new)
    for tile in tiles:
        total = total + jnp.exp(tile - new)
    tops[...] = new
    totals[...] = total

    @pl.when(step == pl.num_programs(0) - 1)
    def _():
        lane_top, lane_total = tops[...], totals[...]
        top = jnp.max(lane_top, axis=1, keepdims=True)
        total = jnp.sum(lane_total * jnp.exp(lane_top - top), axis=1, keepdims=True)
        part = mass_ref.shape[0]
        flat = jnp.transpose(lanes_of((top, total), rows))
        mass = jnp.transpose(mass_ref[...])
        mass = jnp.concatenate([mass[0:1], jnp.zeros((1, rows - part), F32)], axis=1)
        packed = jnp.concatenate([flat[0:2], mass, jnp.zeros((1, rows), F32)], axis=0)
        stats_ref[...] = jnp.concatenate([packed, jnp.zeros((4, rows), F32)], axis=0)


def grad_kernel(
    place_ref, slot_ref, from_ref, stats_refs, logits_ref, target_ref, hidden_ref, hidden_t_ref, weight_ref,
    dweight_ref, dhidden_ref, base_ref, norm, mass, gain, cross, partial, by_place, in_order,
):
    step = pl.program_id(0)
    count, _, part, _ = target_ref.shape
    rows, cols = logits_ref.shape[1:]
    width = weight_ref.shape[1]

    @pl.when(step == 0)
    def _():
        top = functools.reduce(jnp.maximum, [ref[0:1] for ref in stats_refs])
        total = functools.reduce(
            jnp.add, [ref[1:2] * jnp.exp(ref[0:1] - top) for ref in stats_refs]
        )
        norm[...] = jnp.transpose(jnp.broadcast_to(top + jnp.log(total), (LANES, rows)))
        ring = stats_refs[0].shape[0] - 8
        for e, ref in enumerate(stats_refs):
            for k in range(ring):
                by_place[e * ring + k] = ref[8 + k : 9 + k, 0:LANES]
        for t in range(count):
            in_order[t] = by_place[from_ref[t]]
        own = in_order[...][:, 0, :]
        spread = jnp.broadcast_to(own[:, None, :], (count, part, LANES))
        diagonal = lax.broadcasted_iota(jnp.int32, (count, part, LANES), 1) == lax.broadcasted_iota(
            jnp.int32, (count, part, LANES), 2
        )
        column = jnp.sum(jnp.where(diagonal, spread, 0.0), axis=2, keepdims=True).reshape(rows, 1)
        mass[...] = jnp.broadcast_to(column, (rows, LANES))
        gain[...] = jnp.broadcast_to(
            hidden_ref[:, width : width + LANES].astype(F32)[:, 0:1], (rows, LANES)
        )
        cross[...] = jnp.zeros(cross.shape, F32)

    norm_tile, mass_tile, gain_tile = norm[...], mass[...], gain[...]
    crossed = cross[...]
    grads = []
    for q in range(cols // LANES):
        logit = logits_ref[0, :, q * LANES : (q + 1) * LANES]
        slot = slot_ref[step * (cols // LANES) + q]
        held = target_ref[:, jnp.maximum(slot, 0)].reshape(rows, LANES).astype(F32)
        target = jnp.where(slot >= 0, held, 0.0)
        crossed = crossed + target * logit
        grads.append(
            (gain_tile * (mass_tile * jnp.exp(logit - norm_tile) - target)).astype(BF16)
        )
    cross[...] = crossed
    grad = jnp.concatenate(grads, axis=1)
    dweight_ref[0] = jnp.dot(hidden_t_ref[...], grad, preferred_element_type=F32).astype(BF16)
    product = lax.dot_general(
        grad, weight_ref[0], (((1,), (1,)), ((), ())), preferred_element_type=F32
    )

    @pl.when(step == 0)
    def _():
        partial[...] = product

    @pl.when(step > 0)
    def _():
        partial[...] = partial[...] + product

    @pl.when(step == pl.num_programs(0) - 1)
    def _():
        cross_sum = jnp.sum(cross[...], axis=1, keepdims=True)
        cross[...] = lanes_of(pieces(cross_sum), rows)
        for t in range(count):
            c = place_ref[t]
            dhidden_ref[c, :, 0:width] = partial[t * part : (t + 1) * part, :].astype(BF16)
            dhidden_ref[c, :, width : width + LANES] = cross[t * part : (t + 1) * part, :].astype(BF16)
        mass[...] = mass[...] * norm[...]
        start = pl.multiple_of(place_ref[count] * part, part)
        base_ref[...] = mass[pl.ds(start, part), :]


def grads_of(lines):
    def kernel(place_ref, slot_ref, from_ref, *refs):
        grad_kernel(place_ref, slot_ref, from_ref, refs[:lines], *refs[lines:])

    return kernel


def merge_kernel(*refs):
    out_ref = refs[-1]
    top = functools.reduce(jnp.maximum, [ref[0:1] for ref in refs[:-1]])
    total = functools.reduce(jnp.add, [ref[1:2] * jnp.exp(ref[0:1] - top) for ref in refs[:-1]])
    out_ref[0:8] = jnp.concatenate([top, total, jnp.zeros((6, top.shape[1]), F32)], axis=0)
    for k, ref in enumerate(refs[:-1]):
        out_ref[8 + k : 9 + k] = ref[2:3]


def rows_kernel(turned_ref, in_ref, rows_ref, loss_ref):
    count, part, wide = in_ref.shape
    width = wide - LANES
    for v in range(count):
        got = in_ref[(v + turned_ref[0]) % count]
        rows_ref[v * part : (v + 1) * part, :] = got[:, 0:width]
        tail = got[:, width:wide].astype(F32)
        loss_ref[v * part : (v + 1) * part, :] = jnp.broadcast_to(
            tail[:, 0:1] + tail[:, 1:2] + tail[:, 2:3], (part, LANES)
        )


def stack_kernel(*refs):
    out_ref = refs[-1]
    part = refs[0].shape[0]
    for k, ref in enumerate(refs[:-1]):
        out_ref[k * part : (k + 1) * part, :] = ref[...]


def arrange_kernel(behind_ref, *refs):
    out_ref, held = refs[-2:]
    near = refs[0].shape[0]
    for k, ref in enumerate(refs[:-2]):
        held[k * near : (k + 1) * near] = ref[...]
    for t in range(out_ref.shape[0]):
        out_ref[t] = held[behind_ref[t]]


def fold(refs):
    wide = refs[0].shape[-1]
    total = refs[0][...].astype(F32)
    for ref in refs[1:]:
        total = total + ref[...].astype(F32)
    tail = total[:, wide - LANES :]
    return total[:, : wide - LANES], tail[:, 0:1] + tail[:, 1:2] + tail[:, 2:3]


def fold_kernel(*refs):
    out_ref = refs[-1]
    rows, wide = out_ref.shape
    total, crossed = fold(refs[:-1])
    out_ref[:, 0 : wide - LANES] = total.astype(BF16)
    out_ref[:, wide - LANES : wide] = lanes_of(pieces(crossed), rows).astype(BF16)


def finish_kernel(*refs):
    base_ref, out_ref = refs[-2:]
    rows, wide = out_ref.shape
    total, crossed = fold(refs[:-2])
    out_ref[:, 0 : wide - LANES] = total.astype(BF16)
    loss = base_ref[:, 0:1] - crossed
    out_ref[:, wide - LANES : wide] = lanes_of(pieces(loss), rows).astype(BF16)


def whole(shape):
    return pl.BlockSpec(shape, lambda *_: (0,) * len(shape))


def shifted(value, ring, along_x, step):
    count = lax.axis_size("ctx")
    lines = count // ring
    pairs = []
    for x in range(lines):
        for z in range(ring):
            to = (x + step) % lines * ring + z if along_x else x * ring + (z + step) % ring
            pairs.append((x * ring + z, to))
    return lax.ppermute(value, "ctx", pairs)


def spread(value, ring, along_x):
    count = lax.axis_size("ctx") // ring if along_x else ring
    return [value] + [shifted(value, ring, along_x, step) for step in range(1, count)]


def exchange(
    capacity, ring, head_weight, incoming, compact_slot, whole_slot, own_slot, place, behind, from_where, *lines
):
    ctx_count = lax.axis_size("ctx")
    voc_count, held, part, _ = incoming.shape
    width, cols = head_weight.shape
    dev_blocks = cols // LANES
    owned_blocks = voc_count * dev_blocks
    rows = ctx_count * part
    slots = ctx_count * capacity
    wide = width + LANES
    smem = pl.BlockSpec(memory_space=pltpu.SMEM)

    weights = lax.all_gather(head_weight, "voc", axis=0, tiled=False)
    slot = compact_slot if capacity == COMPACT else whole_slot
    target, mass = pl.pallas_call(
        collect_kernel,
        out_shape=(
            jax.ShapeDtypeStruct((slots, part, LANES), BF16),
            jax.ShapeDtypeStruct((part, LANES), F32),
        ),
        in_specs=[smem, pl.BlockSpec(memory_space=pltpu.VMEM)],
        scratch_shapes=[
            pltpu.VMEM((slots, part, LANES), F32),
            pltpu.VMEM((voc_count, part, LANES), F32),
        ],
        compiler_params=params(20),
        cost_estimate=pl.CostEstimate(
            flops=4 * slots * part * LANES, bytes_accessed=6 * 1024 * 1024, transcendentals=0
        ),
        name="collect_targets",
    )(slot, incoming)
    target = target.reshape(ctx_count, capacity, part, LANES)
    arrived = lax.all_to_all(target, "ctx", 0, 0, tiled=True)
    hidden_rows = pl.pallas_call(
        arrange_kernel,
        out_shape=jax.ShapeDtypeStruct((ctx_count, part, wide), BF16),
        in_specs=[smem] + [pl.BlockSpec(memory_space=pltpu.VMEM)] * len(lines),
        scratch_shapes=[pltpu.VMEM((ctx_count, part, wide), BF16)],
        compiler_params=params(),
        name="arrange_rows",
    )(behind, *[line.reshape(ring, part, wide) for line in lines]).reshape(rows, wide)
    hidden_t = hidden_rows[:, :width].T

    logits, stats = pl.pallas_call(
        logits_kernel,
        grid=(voc_count,),
        in_specs=[
            pl.BlockSpec((rows, width), lambda j: (0, 0)),
            pl.BlockSpec((1, width, cols), lambda j: (j, 0, 0)),
            whole((part, LANES)),
        ],
        out_specs=(
            pl.BlockSpec((1, rows, cols), lambda j: (j, 0, 0)),
            whole((8, rows)),
        ),
        out_shape=(
            jax.ShapeDtypeStruct((voc_count, rows, cols), F32),
            jax.ShapeDtypeStruct((8, rows), F32),
        ),
        scratch_shapes=[pltpu.VMEM((rows, LANES), F32)] * 2,
        compiler_params=params(56),
        cost_estimate=pl.CostEstimate(
            flops=2 * rows * width * cols * voc_count,
            bytes_accessed=18 * 1024 * 1024,
            transcendentals=rows * cols * voc_count,
        ),
        name="student_logits",
    )(hidden_rows, weights, mass)
    def merge(parts):
        return pl.pallas_call(
            merge_kernel,
            out_shape=jax.ShapeDtypeStruct((8 + ring, rows), F32),
            compiler_params=params(),
            name="merge_stats",
        )(*parts)

    if capacity == COMPACT:
        all_stats = spread(merge(spread(stats, ring, False)), ring, True)
    else:
        arrived, stats = lax.optimization_barrier((arrived, stats))
        everywhere = jnp.broadcast_to(stats[None], (ctx_count, 8, rows))
        got = lax.all_to_all(everywhere, "ctx", 0, 0, tiled=True)
        all_stats = [
            merge([got[e + k] for k in range(ring)]) for e in range(0, ctx_count, ring)
        ]
        from_where = jnp.arange(ctx_count, dtype=jnp.int32)

    dweight, dhidden, base = pl.pallas_call(
        grads_of(len(all_stats)),
        grid=(voc_count,),
        in_specs=[
            smem,
            smem,
            smem,
        ]
        + [whole((8 + ring, rows))] * len(all_stats)
        + [
            pl.BlockSpec((1, rows, cols), lambda j: (j, 0, 0)),
            whole((ctx_count, capacity, part, LANES)),
            whole((rows, width + LANES)),
            whole((width, rows)),
            pl.BlockSpec((1, width, cols), lambda j: (j, 0, 0)),
        ],
        out_specs=(
            pl.BlockSpec((1, width, cols), lambda j: (j, 0, 0)),
            whole((ctx_count, part, width + LANES)),
            whole((part, LANES)),
        ),
        out_shape=(
            jax.ShapeDtypeStruct((voc_count, width, cols), BF16),
            jax.ShapeDtypeStruct((ctx_count, part, width + LANES), BF16),
            jax.ShapeDtypeStruct((part, LANES), F32),
        ),
        scratch_shapes=[pltpu.VMEM((rows, LANES), F32)] * 4
        + [pltpu.VMEM((rows, width), F32)]
        + [pltpu.VMEM((ctx_count, 1, LANES), F32)] * 2,
        compiler_params=params(48),
        cost_estimate=pl.CostEstimate(
            flops=4 * rows * width * cols * voc_count,
            bytes_accessed=30 * 1024 * 1024,
            transcendentals=rows * cols * voc_count,
        ),
        name="grads",
    )(place, own_slot, from_where, *all_stats, logits, arrived, hidden_rows, hidden_t, weights)
    return dweight, dhidden, base


def local(hidden, token_weight, head_weight, teacher_logits, block_coeff, block_map):
    ctx_count = lax.axis_size("ctx")
    voc_count = lax.axis_size("voc")
    voc_index = lax.axis_index("voc")
    ctx_index = lax.axis_index("ctx")
    rows_dev, width = hidden.shape
    half_rows = rows_dev // 2
    part = rows_dev // voc_count
    half_groups = voc_count // 2
    local_blocks = block_coeff.shape[0]
    cols = head_weight.shape[1]
    dev_blocks = cols // LANES
    owned_blocks = voc_count * dev_blocks
    slots = ctx_count * owned_blocks
    rows = ctx_count * part
    wide = width + LANES

    parity = voc_index // half_groups
    fold_side = jnp.where(ctx_index % 2 == parity, 0, 1)
    start = fold_side * half_rows + voc_index % half_groups * part
    mine = lax.dynamic_slice_in_dim(hidden, start, part, 0)
    mine_weight = lax.dynamic_slice_in_dim(token_weight, start, part, 0)
    mine = jnp.concatenate([mine, jnp.broadcast_to(mine_weight[:, None], (part, LANES))], axis=1)
    ring = min(8, ctx_count)
    outgoing = pl.pallas_call(
        teacher_kernel,
        out_shape=jax.ShapeDtypeStruct((voc_count, local_blocks + 1, part, LANES), BF16),
        compiler_params=params(56),
        cost_estimate=pl.CostEstimate(
            flops=2 * rows_dev * local_blocks * LANES * LANES,
            bytes_accessed=6 * 1024 * 1024,
            transcendentals=rows_dev * local_blocks * LANES,
        ),
        name="teacher_map",
    )(teacher_logits, block_coeff)
    outgoing, mine = lax.optimization_barrier((outgoing, mine))
    near = pl.pallas_call(
        stack_kernel,
        out_shape=jax.ShapeDtypeStruct((ring * part, wide), BF16),
        compiler_params=params(),
        name="stack_rows",
    )(*spread(mine, ring, False))
    incoming = lax.all_to_all(outgoing, "voc", 0, 0, tiled=True)

    wanted = jnp.any(
        block_map[:, None] == jnp.arange(slots, dtype=jnp.int32)[None, :], axis=0
    ).astype(jnp.int32).reshape(ctx_count, owned_blocks)
    number = jnp.cumsum(wanted, axis=1) - wanted
    fits = jnp.max(jnp.sum(wanted, axis=1)) <= COMPACT
    own_slot = jnp.where(wanted == 1, number, -1)
    own_slot = lax.dynamic_index_in_dim(own_slot, ctx_index, 0, keepdims=False)
    in_order = number.reshape(slots)[block_map]
    compact_slot = block_map // owned_blocks * COMPACT + in_order
    whole_slot = block_map // owned_blocks * owned_blocks + in_order

    source = jnp.arange(ctx_count, dtype=jnp.int32)
    half_block = 2 * source + parity
    place = jnp.where(half_block < ctx_count, half_block, 2 * ctx_count - 1 - half_block)
    own_half = jnp.where(fold_side == 0, ctx_index, 2 * ctx_count - 1 - ctx_index)
    behind = (ctx_index // ring - place // ring) % (ctx_count // ring) * ring + (ctx_index - place) % ring
    from_where = (ctx_index // ring - source // ring) % (ctx_count // ring) * ring + (
        ctx_index - source
    ) % ring
    ahead = (place // ring - ctx_index // ring) % (ctx_count // ring) * ring + (place - ctx_index) % ring
    place = jnp.concatenate([ahead, (own_half // 2)[None]]).astype(jnp.int32)
    lines = spread(near, ring, True)
    operands = lax.optimization_barrier(
        (incoming, compact_slot, whole_slot, own_slot, place, behind, from_where, *lines)
    )
    dweight, dhidden, base = lax.cond(
        fits,
        functools.partial(exchange, COMPACT, ring),
        functools.partial(exchange, owned_blocks, ring),
        head_weight,
        *operands,
    )
    grad_weight = lax.psum_scatter(dweight, "voc", scatter_dimension=0, tiled=True)
    grad_weight = grad_weight.reshape(width, cols).astype(F32)
    pieces_x = dhidden.reshape(ctx_count // ring, ring * part, wide)
    parts = [pieces_x[0]]
    parts += [shifted(pieces_x[e], ring, True, e) for e in range(1, ctx_count // ring)]
    folded = pl.pallas_call(
        fold_kernel,
        out_shape=jax.ShapeDtypeStruct((ring * part, wide), BF16),
        compiler_params=params(),
        name="fold_rows",
    )(*parts)
    pieces_z = folded.reshape(ring, part, wide)
    parts = [pieces_z[0]] + [shifted(pieces_z[e], ring, False, e) for e in range(1, ring)]
    done = pl.pallas_call(
        finish_kernel,
        out_shape=jax.ShapeDtypeStruct((part, wide), BF16),
        compiler_params=params(),
        name="finish_rows",
    )(*parts, base)
    all_done = lax.all_gather(done, "voc", axis=0, tiled=False)
    turned = (ctx_index % 2 * half_groups).astype(jnp.int32)
    grad_hidden, loss_tile = pl.pallas_call(
        rows_kernel,
        in_specs=[
            pl.BlockSpec(memory_space=pltpu.SMEM),
            pl.BlockSpec(memory_space=pltpu.VMEM),
        ],
        out_shape=(
            jax.ShapeDtypeStruct((rows_dev, width), BF16),
            jax.ShapeDtypeStruct((rows_dev, LANES), F32),
        ),
        compiler_params=params(),
        name="own_rows",
    )(turned[None], all_done)
    row_loss = loss_tile[:, 0]
    return (grad_hidden, grad_weight, row_loss)


def solution(mesh):
    return jax.shard_map(
        local,
        mesh=mesh,
        in_specs=(
            P("ctx", None),
            P("ctx"),
            P(None, ("ctx", "voc")),
            P("ctx", "voc"),
            P("voc", None, None),
            P(),
        ),
        out_specs=(P("ctx", None), P(None, ("ctx", "voc")), P("ctx")),
        check_vma=False,
    )
```
